768 devices in a mesh: row: 192 (over z, y, core), col: 4 (over x).
Axes of the slice: x: 4, y: 8, z: 12, core: 2. Of those that a mesh axis runs over, the one named last changes fastest.
Arguments:
- charges: bfloat16 [768, 128, 256], P('row'), may hold values from -6 to 6
- cluster_basis: bfloat16 [768, 32, 256], P('row'), may hold values from -0.375 to 0.375
- cluster_sizes: int32 [768], P('row'), may hold values from 128 to 256, as said below
- near_blocks: bfloat16 [12288, 256, 256], P(('row', 'col')), may hold values from -0.09375 to 0.09375
- near_rows: int32 [12288], P(('row', 'col')), may hold values from 0 to 767, as said below
- near_cols: int32 [12288], P(('row', 'col')), may hold values from 0 to 767, as said below
- near_live: int32 [768], P(('row', 'col')), may hold values from 1 to 16, as said below
- couplings: bfloat16 [98304, 32, 32], P(('row', 'col')), may hold values from -0.25 to 0.25
- far_rows: int32 [98304], P(('row', 'col')), may hold values from 0 to 767, as said below
- far_cols: int32 [98304], P(('row', 'col')), may hold values from 0 to 767, as said below
- far_live: int32 [768], P(('row', 'col')), may hold values from 0 to 128, as said below
Outputs:
- first_image: bfloat16 [768, 128, 256], P('row')
- second_image: bfloat16 [768, 128, 256], P('row')
The draws below stay inside these ranges and needn't reach their ends.
Inputs may be any that keep to these rules, and one draw needn't show every extreme that they name: `cluster_sizes`: in every block of 4 clusters of one row index, some cluster uses all 256 panels. `near_rows`: slot s belongs to device s // 16, devices counted with row slowest and col fastest; its row cluster lies among the 4 clusters of that device's row index. `near_cols`: for a slot in use whose row cluster i lies in the block that starts at cluster b, the column cluster is at least i and below b + 8. Slots not in use hold any cluster. `near_live`: the used slots are the device's first ones. In each row index, one device uses all 16. `far_rows`: slot s belongs to device s // 128, devices counted with row slowest and col fastest; its row cluster lies among the 4 clusters of that device's row index. `far_cols`: for a slot in use whose row cluster lies in the block that starts at cluster b, the column cluster is at least b + 4 and below b + 32. Slots not in use hold any cluster. `far_live`: the used slots are the device's first ones. Devices of the last row index use none; in every other row index one device uses all 128.
All inputs are finite; a program needn't handle non-finite values.
Results may differ from the reference program's by a relative error of at most 0.022.
Values may be sent and summed in bfloat16 or wider, within the bound.
A program may use at most 64 MiB of HBM per device.

```python
import jax
import jax.numpy as jnp
from jax import lax

PANELS = 256
RANK = 32
RHS = 128
CLUSTERS_DEV = 4
NEAR = 16
FAR = 128
FAR_SLABS = 8
CLUSTERS = 768
NEAR_SLOTS = 12288
FAR_SLOTS = 98304


def layout_counts():
    row_count = CLUSTERS // CLUSTERS_DEV
    col_count = NEAR_SLOTS // NEAR // row_count
    return (row_count, col_count)


def near_lists(key):
    key = jax.random.fold_in(key, 101)
    row_count, col_count = layout_counts()
    slot_ids = jnp.arange(NEAR_SLOTS, dtype=jnp.int32)
    slab_ids = slot_ids // (NEAR * col_count)
    row_key, col_key = jax.random.split(key)
    row_ids = slab_ids * CLUSTERS_DEV + jax.random.randint(row_key, (NEAR_SLOTS,), 0, CLUSTERS_DEV, dtype=jnp.int32)
    limits = jnp.minimum((slab_ids + 2) * CLUSTERS_DEV, CLUSTERS)
    col_ids = row_ids + jax.random.randint(col_key, (NEAR_SLOTS,), 0, limits - row_ids, dtype=jnp.int32)
    return (row_ids, col_ids)


def far_lists(key):
    key = jax.random.fold_in(key, 202)
    row_count, col_count = layout_counts()
    slot_ids = jnp.arange(FAR_SLOTS, dtype=jnp.int32)
    slab_ids = slot_ids // (FAR * col_count)
    row_key, col_key = jax.random.split(key)
    row_ids = slab_ids * CLUSTERS_DEV + jax.random.randint(row_key, (FAR_SLOTS,), 0, CLUSTERS_DEV, dtype=jnp.int32)
    first_ahead = (slab_ids + 1) * CLUSTERS_DEV
    spans = jnp.maximum(jnp.minimum((slab_ids + FAR_SLABS) * CLUSTERS_DEV, CLUSTERS) - first_ahead, 1)
    col_ids = jnp.minimum(first_ahead + jax.random.randint(col_key, (FAR_SLOTS,), 0, spans, dtype=jnp.int32), CLUSTERS - 1)
    return (row_ids, col_ids)


def busy_counts(key, most, row_count, col_count):
    busy_key, other_key = jax.random.split(key)
    busiest = jax.random.randint(busy_key, (row_count,), 0, col_count, dtype=jnp.int32)
    others = jax.random.randint(other_key, (row_count, col_count), 1, most // 2 + 1, dtype=jnp.int32)
    full_device = jnp.arange(col_count, dtype=jnp.int32)[None, :] == busiest[:, None]
    return jnp.where(full_device, most, others)


def draw_cluster_sizes(key, part):
    key = jax.random.fold_in(key, 5)
    row_count, col_count = layout_counts()
    size_key, pick_key = jax.random.split(key)
    sizes = jax.random.randint(size_key, (CLUSTERS,), PANELS // 2, PANELS + 1, dtype=jnp.int32)
    picked = jax.random.randint(pick_key, (row_count,), 0, CLUSTERS_DEV, dtype=jnp.int32)
    full_cluster = jnp.arange(CLUSTERS, dtype=jnp.int32) % CLUSTERS_DEV == jnp.repeat(picked, CLUSTERS_DEV)
    return jnp.where(full_cluster, PANELS, sizes).astype(jnp.int32)


def draw_near_rows(key, part):
    pair_lists = near_lists(key)
    return pair_lists[0]


def draw_near_cols(key, part):
    pair_lists = near_lists(key)
    return pair_lists[1]


def draw_far_rows(key, part):
    pair_lists = far_lists(key)
    return pair_lists[0]


def draw_far_cols(key, part):
    pair_lists = far_lists(key)
    return pair_lists[1]


def draw_near_live(key, part):
    key = jax.random.fold_in(key, 7)
    row_count, col_count = layout_counts()
    return busy_counts(key, NEAR, row_count, col_count).reshape(-1).astype(jnp.int32)


def draw_far_live(key, part):
    key = jax.random.fold_in(key, 9)
    row_count, col_count = layout_counts()
    counts = busy_counts(key, FAR, row_count, col_count)
    last_row = jnp.arange(row_count, dtype=jnp.int32)[:, None] == row_count - 1
    return jnp.where(last_row, 0, counts).reshape(-1).astype(jnp.int32)


def steps_of(key, shape, shards, smallest, largest):
    def one(axis_at, parts):
        draws = jax.random.uniform(jax.random.fold_in(jax.random.fold_in(key, 6), axis_at), (parts,), jnp.float32, smallest / len(shards), largest / len(shards))
        return jnp.repeat(jnp.exp(draws), shape[axis_at] // parts).reshape((-1,) + (1,) * (len(shape) - axis_at - 1))

    gain = one(*shards[0])
    for cut in shards[1:]:
        gain = gain * one(*cut)
    return gain


def noise(key, extent, width, limit, cuts=(), kind=jnp.bfloat16):
    entries = jax.random.normal(key, extent, jnp.float32) * width
    if len(cuts) > 0:
        entries = steps_of(key, extent, cuts, -0.22, 0.18) * entries
    return jnp.clip(entries, min=-limit, max=limit).astype(kind)


def setup_inputs(seed: int = 0) -> dict:
    splits = jax.random.split(jax.random.key(seed), 12)
    charges = noise(splits[0], (CLUSTERS, RHS, PANELS), 1.0, 6.0, ((0, 192),))
    cluster_basis = noise(splits[1], (CLUSTERS, RANK, PANELS), PANELS ** -0.5, 0.375, ((0, 192),))
    cluster_sizes = draw_cluster_sizes(jax.random.fold_in(splits[11], 71), 0)
    near_blocks = noise(splits[3], (NEAR_SLOTS, PANELS, PANELS), (16 * PANELS) ** -0.5, 0.09375, ((0, 768),))
    near_rows = draw_near_rows(jax.random.fold_in(splits[11], 71), 0)
    near_cols = draw_near_cols(jax.random.fold_in(splits[11], 71), 0)
    near_live = draw_near_live(jax.random.fold_in(splits[11], 71), 0)
    couplings = noise(splits[7], (FAR_SLOTS, RANK, RANK), (16 * RANK) ** -0.5, 0.25, ((0, 768),))
    far_rows = draw_far_rows(jax.random.fold_in(splits[11], 71), 0)
    far_cols = draw_far_cols(jax.random.fold_in(splits[11], 71), 0)
    far_live = draw_far_live(jax.random.fold_in(splits[11], 71), 0)
    return {"charges": charges, "cluster_basis": cluster_basis, "cluster_sizes": cluster_sizes, "near_blocks": near_blocks, "near_rows": near_rows, "near_cols": near_cols, "near_live": near_live, "couplings": couplings, "far_rows": far_rows, "far_cols": far_cols, "far_live": far_live}


highest = lax.Precision.HIGHEST


def slot_used(live_numbers, per_device):
    slot_ids = jnp.arange(live_numbers.shape[0] * per_device, dtype=jnp.int32)
    return ((slot_ids % per_device) < live_numbers[slot_ids // per_device]).astype(jnp.float32)


def apply_operator(vector_field, cluster_basis, panel_mask, near_blocks, near_rows, near_cols, near_used, couplings, far_rows, far_cols, far_used):
    coefficients = jnp.einsum("crp,ckp->crk", cluster_basis.astype(jnp.float32), vector_field.astype(jnp.float32), precision=highest).astype(jnp.bfloat16)

    def near_device(totals, pieces):
        blocks, row_ids, col_ids, in_use = pieces
        blocks = blocks.astype(jnp.float32)
        forward = jnp.einsum("spq,skq->skp", blocks, vector_field[col_ids].astype(jnp.float32), precision=highest)
        backward = jnp.einsum("spq,skp->skq", blocks, vector_field[row_ids].astype(jnp.float32), precision=highest)
        totals = totals.at[row_ids].add(forward * in_use[:, None, None])
        totals = totals.at[col_ids].add(backward * in_use[:, None, None])
        return totals, None

    near_sum, _ = lax.scan(near_device, jnp.zeros(vector_field.shape, jnp.float32), (near_blocks.reshape(-1, NEAR, PANELS, PANELS), near_rows.reshape(-1, NEAR), near_cols.reshape(-1, NEAR), near_used.reshape(-1, NEAR)))

    def far_device(totals, pieces):
        matrices, row_ids, col_ids, in_use = pieces
        matrices = matrices.astype(jnp.float32)
        forward = jnp.einsum("frt,ftk->frk", matrices, coefficients[col_ids].astype(jnp.float32), precision=highest)
        backward = jnp.einsum("ftr,ftk->frk", matrices, coefficients[row_ids].astype(jnp.float32), precision=highest)
        totals = totals.at[row_ids].add(forward * in_use[:, None, None])
        totals = totals.at[col_ids].add(backward * in_use[:, None, None])
        return totals, None

    far_sum, _ = lax.scan(far_device, jnp.zeros((CLUSTERS, RANK, RHS), jnp.float32), (couplings.reshape(-1, FAR, RANK, RANK), far_rows.reshape(-1, FAR), far_cols.reshape(-1, FAR), far_used.reshape(-1, FAR)))
    far_rounded = far_sum.astype(jnp.bfloat16)
    new_image = near_sum + jnp.einsum("crp,crk->ckp", cluster_basis.astype(jnp.float32), far_rounded.astype(jnp.float32), precision=highest)
    return jnp.where(panel_mask, new_image, jnp.zeros_like(new_image)).astype(jnp.bfloat16)


def reference(charges, cluster_basis, cluster_sizes, near_blocks, near_rows, near_cols, near_live, couplings, far_rows, far_cols, far_live):
    panel_mask = jnp.arange(PANELS, dtype=jnp.int32)[None, None, :] < cluster_sizes[:, None, None]
    masked = jnp.where(panel_mask, charges, jnp.zeros_like(charges))
    near_used = slot_used(near_live, NEAR)
    far_used = slot_used(far_live, FAR)
    first_image = apply_operator(masked, cluster_basis, panel_mask, near_blocks, near_rows, near_cols, near_used, couplings, far_rows, far_cols, far_used)
    second_image = apply_operator(first_image, cluster_basis, panel_mask, near_blocks, near_rows, near_cols, near_used, couplings, far_rows, far_cols, far_used)
    return (first_image, second_image)
```

```python
import functools

import jax
import jax.numpy as jnp
from jax import lax
from jax.experimental import pallas as pl
from jax.experimental.pallas import tpu as pltpu
from jax.sharding import PartitionSpec as P

MESH = pl.DeviceIdType.MESH
F32 = jnp.float32
BF16 = jnp.bfloat16
I32 = jnp.int32

SLAB = 4
REACH = 7
NEAR = 16
FAR = 128
RANK = 32
RHS = 128
PANELS = 256
LANES = 128

FIELD, COEF, AHEAD, PART, FARPART, FARBACK, IMAGE, PER_APPLY = 0, 4, 11, 15, 18, 21, 28, 31
DENSE = 2 * PER_APPLY
N_SEMS = DENSE + 3


def sort_keys(unique_keys):
    across = jnp.broadcast_to(unique_keys, (LANES, LANES))
    down = across.T
    rank = jnp.sum(jnp.where(across < down, 1, 0).astype(I32), axis=1, keepdims=True)
    lane = lax.broadcasted_iota(I32, (LANES, LANES), 1)
    ordered = jnp.sum(jnp.where(rank == lane, down, 0), axis=0, keepdims=True)
    return ordered, down


def count_upto(down, shift):
    lane = lax.broadcasted_iota(I32, (LANES, LANES), 1)
    return jnp.sum(jnp.where((down >> shift) <= lane, 1, 0).astype(I32), axis=0, keepdims=True)


def kernel(
    n_rows,
    charges_hbm,
    basis_ref,
    sizes_ref,
    blocks_hbm,
    near_rows_ref,
    near_cols_ref,
    near_live_ref,
    couplings_hbm,
    far_rows_ref,
    far_cols_ref,
    far_live_ref,
    out1_hbm,
    out2_hbm,
    charges,
    blocks,
    couplings,
    own_first,
    own_second,
    next_first,
    next_second,
    final,
    order_v,
    order_s,
    coef_own,
    coef_ahead,
    spread,
    far_prefix,
    dense_send,
    dense_recv,
    dense,
    near_prefix,
    back_prefix,
    ahead_send,
    ahead_recv,
    part_send,
    part_recv,
    farpart_send,
    farpart_recv,
    farback_send,
    farback_recv,
    send_sem,
    recv_sem,
    load_sem,
):
    r = lax.axis_index("row")
    c = lax.axis_index("col")
    own = (own_first, own_second)
    ahead = (next_first, next_second)

    def up(o):
        return (lax.rem(r + o, n_rows), c)

    def down(o):
        return (lax.rem(r + n_rows - o, n_rows), c)

    def beside(d):
        return (r, lax.rem(c + d, SLAB))

    def remote(src, dst, at, device):
        return pltpu.make_async_remote_copy(
            src_ref=src,
            dst_ref=dst,
            send_sem=send_sem.at[at],
            recv_sem=recv_sem.at[at],
            device_id=device,
            device_id_type=MESH,
        )

    load_charges = pltpu.make_async_copy(charges_hbm, charges, load_sem.at[0])
    load_couplings = pltpu.make_async_copy(couplings_hbm, couplings, load_sem.at[1])
    load_blocks = pltpu.make_async_copy(blocks_hbm, blocks, load_sem.at[2])
    load_charges.start()
    load_couplings.start()
    load_blocks.start()

    barrier = pltpu.get_barrier_semaphore()
    peers = [up(o) for o in range(1, REACH + 1)]
    peers += [down(o) for o in range(1, REACH + 1)]
    peers += [beside(d) for d in range(1, SLAB)]
    for peer in peers:
        pl.semaphore_signal(barrier, inc=1, device_id=peer, device_id_type=MESH)

    first = r * SLAB
    lane = lax.broadcasted_iota(I32, (1, LANES), 1)
    near_used = near_live_ref[0]
    by_row = jnp.broadcast_to((1 << 16) + lane, (1, LANES))
    by_col = by_row
    for s in range(NEAR):
        row = jnp.clip(near_rows_ref[s] - first, 0, SLAB - 1)
        col = jnp.clip(near_cols_ref[s] - first, 0, 2 * SLAB - 1)
        used = s < near_used
        row_key = (jnp.where(used, row, SLAB) << 7) + (col << 4) + s
        col_key = (jnp.where(used, col, 2 * SLAB) << 7) + (row << 4) + s
        by_row = jnp.where(lane == s, row_key, by_row)
        by_col = jnp.where(lane == s, col_key, by_col)
    far_row = jnp.clip(far_rows_ref[...] - first, 0, SLAB - 1).reshape(1, LANES)
    far_col = jnp.clip(far_cols_ref[...] - first - SLAB, 0, REACH * SLAB - 1).reshape(1, LANES)
    far_slab = far_col >> 2
    far_group = ((far_col & 3) * SLAB + far_row) * 2 + (far_slab >> 2)
    far_group = jnp.where(lane < far_live_ref[0], far_group, 2 * SLAB * SLAB)
    by_tile = ((far_group * 4 + (far_slab & 3)) << 7) + lane
    for at, (keys, shift) in enumerate(((by_row, 7), (by_col, 7), (by_tile, 9))):
        ordered, laid = sort_keys(keys)
        order_v[2 * at : 2 * at + 1, :] = ordered
        order_v[2 * at + 1 : 2 * at + 2, :] = count_upto(laid, shift)
    order_v[6:8, :] = jnp.zeros((2, LANES), I32)
    share_order = pltpu.make_async_copy(order_v, order_s, load_sem.at[3])
    share_order.start()

    panel = lax.broadcasted_iota(I32, (RHS, PANELS), 1)

    def masked(values, size):
        return jnp.where(panel < size, values, jnp.zeros_like(values))

    def last_of(row, group):
        upto = order_s[row, group]
        before = order_s[row, group - 1] if group > 0 else 0
        return jnp.maximum(upto - 1, 0), (upto > before).astype(F32)

    def coefficients(a, i):
        return lax.dot_general(
            basis_ref[i], own[a][i], (((1,), (1,)), ((), ())), preferred_element_type=F32
        ).astype(BF16)

    def own_coefficients(a):
        for i in range(SLAB):
            coef_own[a, i * RANK : (i + 1) * RANK, :] = coefficients(a, i)

    def near_pass(a, order_row, forward, prefix):
        def slot(k, carry):
            total, previous = carry
            key = order_s[order_row, k]
            group = key >> 7
            other = (key >> 4) & 7
            source = own[a][other & 3]
            if forward:
                source = jnp.where(other < SLAB, source, ahead[a][other & 3])
            block = blocks[key & 15]
            product = lax.dot_general(
                source,
                block,
                (((1,), (1 if forward else 0,)), ((), ())),
                preferred_element_type=F32,
            )
            total = total * (group == previous).astype(F32) + product
            prefix[k] = total
            return total, group

        lax.fori_loop(0, NEAR, slot, (jnp.zeros((RHS, PANELS), F32), jnp.int32(-1)))

    def send_coefficients(a):
        copies = []
        mine = coef_own.at[a, pl.ds(pl.multiple_of(c * RANK, RANK), RANK), :]
        for o in range(1, REACH + 1):
            copy = remote(
                mine,
                coef_ahead.at[a, (o - 1) * RANK : o * RANK, :],
                a * PER_APPLY + COEF + o - 1,
                down(o),
            )
            copy.start()
            copies.append(copy)
        return copies

    sent = []
    for a in range(2):
        coef_ahead[a, REACH * RANK :, :] = jnp.zeros((RANK, RHS), BF16)
    load_charges.wait()
    for i in range(SLAB):
        own_first[i] = masked(charges[i], sizes_ref[i])
    own_coefficients(0)

    pl.semaphore_wait(barrier, len(peers))

    field_copies = [
        remote(own_first.at[i], next_first.at[i], FIELD + i, down(1)) for i in range(SLAB)
    ]
    for copy in field_copies:
        copy.start()
    coef_copies = send_coefficients(0)

    load_couplings.wait()
    share_order.wait()
    rank_at = lax.broadcasted_iota(I32, (RANK, LANES), 0)
    lane_at = lax.broadcasted_iota(I32, (RANK, LANES), 1)
    repeat = jnp.where((lane_at & (RANK - 1)) == rank_at, 1.0, 0.0).astype(BF16)

    def spread_some(n, _):
        some = couplings[pl.ds(n * 16, 16)].reshape(16 * RANK, RANK)
        spread[pl.ds(n * 16, 16)] = jnp.dot(
            some, repeat, preferred_element_type=F32
        ).reshape(16, RANK, LANES)
        return 0

    lax.fori_loop(0, FAR // 16, spread_some, 0)

    def far_slot(k, carry):
        total, previous = carry
        key = order_s[4, k]
        group = key >> 9
        kept = jnp.where((lane_at >> 5) == ((key >> 7) & 3), spread[key & 127], 0.0)
        total = total * (group == previous).astype(F32) + kept
        far_prefix[k] = total
        return total, group

    lax.fori_loop(0, FAR, far_slot, (jnp.zeros((RANK, LANES), F32), jnp.int32(-1)))
    for g in range(2 * SLAB * SLAB):
        at, live = last_of(5, g)
        i, half = (g // 2) % SLAB, g % 2
        dense_send[
            g // (2 * SLAB), i * RANK : (i + 1) * RANK, half * LANES : (half + 1) * LANES
        ] = (far_prefix[at] * live).astype(BF16)
    dense_copies = []
    for d in (2, 1, 3):
        copy = remote(
            dense_send.at[lax.rem(c + d, SLAB)], dense_recv.at[d - 1], DENSE + d - 1, beside(d)
        )
        copy.start()
        dense_copies.append(copy)

    load_blocks.wait()

    for a in range(2):
        base = a * PER_APPLY
        near_pass(a, 2, False, back_prefix)
        for j in range(SLAB):
            at, live = last_of(3, SLAB + j)
            ahead_send[a, j] = (back_prefix[at] * live).astype(BF16)
        ahead_copies = [
            remote(ahead_send.at[a, j], ahead_recv.at[a, j], base + AHEAD + j, up(1))
            for j in range(SLAB)
        ]
        for copy in ahead_copies:
            copy.start()

        if a == 0:
            for copy in dense_copies:
                copy.wait_recv()
            total = dense_send[c].astype(F32)
            for d in range(SLAB - 1):
                total = total + dense_recv[d].astype(F32)
            dense[...] = total.astype(BF16)
        back = lax.dot_general(
            dense[...], coef_own[a], (((0,), (0,)), ((), ())), preferred_element_type=F32
        )
        farback_send[a] = back.astype(BF16)
        farback_copies = []
        for o in range(1, REACH + 1):
            copy = remote(
                farback_send.at[a, (o - 1) * RANK : o * RANK, :],
                farback_recv.at[a, o - 1],
                base + FARBACK + o - 1,
                up(o),
            )
            copy.start()
            farback_copies.append(copy)
        for copy in coef_copies:
            copy.wait_recv()
        farpart_send[a] = jnp.dot(
            dense[...], coef_ahead[a], preferred_element_type=F32
        ).astype(BF16)
        farpart_copies = []
        for d in (2, 1, 3):
            other = lax.rem(c + d, SLAB)
            copy = remote(
                farpart_send.at[a, pl.ds(pl.multiple_of(other * RANK, RANK), RANK), :],
                farpart_recv.at[a, d - 1],
                base + FARPART + d - 1,
                beside(d),
            )
            copy.start()
            farpart_copies.append(copy)

        for copy in field_copies:
            copy.wait_recv()
        near_pass(a, 0, True, near_prefix)
        for copy in ahead_copies:
            copy.wait_recv()

        def own_near(i):
            upto = order_s[1, i]
            before = jnp.where(i > 0, order_s[1, jnp.maximum(i - 1, 0)], 0)
            forward = near_prefix[jnp.maximum(upto - 1, 0)] * (upto > before).astype(F32)
            upto = order_s[3, i]
            before = jnp.where(i > 0, order_s[3, jnp.maximum(i - 1, 0)], 0)
            backward = back_prefix[jnp.maximum(upto - 1, 0)] * (upto > before).astype(F32)
            return forward + backward + ahead_recv[a, i].astype(F32)

        part_copies = []
        for d in (2, 1, 3):
            part_send[a, d - 1] = own_near(lax.rem(c + d, SLAB)).astype(BF16)
            copy = remote(
                part_send.at[a, d - 1], part_recv.at[a, d - 1], base + PART + d - 1, beside(d)
            )
            copy.start()
            part_copies.append(copy)
        image = own_near(c)

        for copy in farpart_copies + farback_copies:
            copy.wait_recv()
        far_total = farpart_send[a, pl.ds(pl.multiple_of(c * RANK, RANK), RANK), :].astype(F32)
        for d in range(SLAB - 1):
            far_total = far_total + farpart_recv[a, d].astype(F32)
        for o in range(REACH):
            far_total = far_total + farback_recv[a, o].astype(F32)
        image = image + lax.dot_general(
            far_total.astype(BF16),
            basis_ref[c],
            (((0,), (0,)), ((), ())),
            preferred_element_type=F32,
        )
        for copy in part_copies:
            copy.wait_recv()
        for d in range(SLAB - 1):
            image = image + part_recv[a, d].astype(F32)
        image = masked(image, sizes_ref[c]).astype(BF16)

        target = own_second if a == 0 else final
        target[c] = image
        image_copies = []
        for d in (2, 1, 3):
            copy = remote(target.at[c], target.at[c], base + IMAGE + d - 1, beside(d))
            copy.start()
            image_copies.append(copy)
        sent += ahead_copies + farback_copies + farpart_copies + part_copies + image_copies
        sent += field_copies + coef_copies
        if a == 0:
            coef_own[1, pl.ds(pl.multiple_of(c * RANK, RANK), RANK), :] = coefficients(1, c)
            relay = remote(own_second.at[c], next_second.at[c], PER_APPLY + FIELD, down(1))
            relay.start()
            field_copies = [relay]
            coef_copies = send_coefficients(1)
            for at, d in ((1, 1), (2, 3), (0, 2)):
                image_copies[at].wait_recv()
                source = lax.rem(c + SLAB - d, SLAB)
                relay = remote(
                    own_second.at[source], next_second.at[source], PER_APPLY + FIELD + d, down(1)
                )
                relay.start()
                field_copies.append(relay)
                coef_own[1, pl.ds(pl.multiple_of(source * RANK, RANK), RANK), :] = coefficients(
                    1, source
                )
            store_first = pltpu.make_async_copy(own_second, out1_hbm, load_sem.at[4])
            store_first.start()
        else:
            for copy in image_copies:
                copy.wait_recv()
            store_second = pltpu.make_async_copy(final, out2_hbm, load_sem.at[5])
            store_second.start()
    for copy in sent + dense_copies:
        copy.wait_send()
    store_first.wait()
    store_second.wait()


def per_device(n_rows, *arrays):
    smem = pl.BlockSpec(memory_space=pltpu.SMEM)
    vmem = pl.BlockSpec(memory_space=pltpu.VMEM)
    hbm = pl.BlockSpec(memory_space=pl.ANY)
    image = jax.ShapeDtypeStruct((SLAB, RHS, PANELS), BF16)
    return pl.pallas_call(
        functools.partial(kernel, n_rows),
        out_shape=(image, image),
        in_specs=[hbm, vmem, smem, hbm, smem, smem, smem, hbm, vmem, vmem, smem],
        out_specs=(hbm, hbm),
        scratch_shapes=[
            pltpu.VMEM((SLAB, RHS, PANELS), BF16),
            pltpu.VMEM((NEAR, PANELS, PANELS), BF16),
            pltpu.VMEM((FAR, RANK, RANK), BF16),
            pltpu.VMEM((SLAB, RHS, PANELS), BF16),
            pltpu.VMEM((SLAB, RHS, PANELS), BF16),
            pltpu.VMEM((SLAB, RHS, PANELS), BF16),
            pltpu.VMEM((SLAB, RHS, PANELS), BF16),
            pltpu.VMEM((SLAB, RHS, PANELS), BF16),
            pltpu.VMEM((8, LANES), I32),
            pltpu.SMEM((8, LANES), I32),
            pltpu.VMEM((2, SLAB * RANK, RHS), BF16),
            pltpu.VMEM((2, (REACH + 1) * RANK, RHS), BF16),
            pltpu.VMEM((FAR, RANK, LANES), F32),
            pltpu.VMEM((FAR, RANK, LANES), F32),
            pltpu.VMEM((SLAB, SLAB * RANK, 2 * LANES), BF16),
            pltpu.VMEM((SLAB - 1, SLAB * RANK, 2 * LANES), BF16),
            pltpu.VMEM((SLAB * RANK, 2 * LANES), BF16),
            pltpu.VMEM((NEAR, RHS, PANELS), F32),
            pltpu.VMEM((NEAR, RHS, PANELS), F32),
            pltpu.VMEM((2, SLAB, RHS, PANELS), BF16),
            pltpu.VMEM((2, SLAB, RHS, PANELS), BF16),
            pltpu.VMEM((2, SLAB - 1, RHS, PANELS), BF16),
            pltpu.VMEM((2, SLAB - 1, RHS, PANELS), BF16),
            pltpu.VMEM((2, SLAB * RANK, RHS), BF16),
            pltpu.VMEM((2, SLAB - 1, RANK, RHS), BF16),
            pltpu.VMEM((2, (REACH + 1) * RANK, RHS), BF16),
            pltpu.VMEM((2, REACH, RANK, RHS), BF16),
            pltpu.SemaphoreType.DMA((N_SEMS,)),
            pltpu.SemaphoreType.DMA((N_SEMS,)),
            pltpu.SemaphoreType.DMA((6,)),
        ],
        compiler_params=pltpu.CompilerParams(
            collective_id=0, has_side_effects=True, vmem_limit_bytes=40 * 1024 * 1024
        ),
    )(*arrays)


def solution(mesh):
    placed = (
        P("row", None, None),
        P("row", None, None),
        P("row"),
        P(("row", "col"), None, None),
        P(("row", "col")),
        P(("row", "col")),
        P(("row", "col")),
        P(("row", "col"), None, None),
        P(("row", "col")),
        P(("row", "col")),
        P(("row", "col")),
    )
    return jax.shard_map(
        functools.partial(per_device, mesh.shape["row"]),
        mesh=mesh,
        in_specs=placed,
        out_specs=(P("row", None, None), P("row", None, None)),
        check_vma=False,
    )
```

```python
import functools

import jax
import jax.numpy as jnp
from jax import lax
from jax.experimental import pallas as pl
from jax.experimental.pallas import tpu as pltpu
from jax.sharding import PartitionSpec as P

MESH = pl.DeviceIdType.MESH
F32 = jnp.float32
BF16 = jnp.bfloat16
I32 = jnp.int32

SLAB = 4
REACH = 7
NEAR = 16
FAR = 128
RANK = 32
RHS = 128
PANELS = 256
LANES = 128
UNROLL = 8

FIELD, COEF, AHEAD, PART, FARPART, FARBACK, IMAGE, PER_APPLY = 0, 4, 11, 15, 18, 21, 28, 31
DENSE = 2 * PER_APPLY
N_SEMS = DENSE + 3
TURNS = (2, 1, 3, 0)


def sort_keys(unique_keys):
    across = jnp.broadcast_to(unique_keys, (LANES, LANES))
    down = across.T
    rank = jnp.sum(jnp.where(across < down, 1, 0).astype(I32), axis=1, keepdims=True)
    lane = lax.broadcasted_iota(I32, (LANES, LANES), 1)
    ordered = jnp.sum(jnp.where(rank == lane, down, 0), axis=0, keepdims=True)
    return ordered, down


def count_upto(down, shift):
    lane = lax.broadcasted_iota(I32, (LANES, LANES), 1)
    return jnp.sum(jnp.where((down >> shift) <= lane, 1, 0).astype(I32), axis=0, keepdims=True)


def kernel(
    n_rows,
    charges_hbm,
    basis_hbm,
    sizes_hbm,
    blocks_hbm,
    near_rows_hbm,
    near_cols_hbm,
    near_live_hbm,
    couplings_hbm,
    far_rows_hbm,
    far_cols_hbm,
    far_live_hbm,
    first_image,
    second_image,
    charges,
    basis_ref,
    sizes_ref,
    blocks,
    near_rows_ref,
    near_cols_ref,
    near_live_ref,
    couplings,
    far_rows_ref,
    far_cols_ref,
    far_live_ref,
    masked_charges,
    next_first,
    next_second,
    order_v,
    order_s,
    coef_own,
    coef_ahead,
    dense_sum,
    dense_send,
    dense_recv,
    dense,
    near_prefix,
    back_prefix,
    ahead_send,
    ahead_recv,
    part_send,
    part_recv,
    farpart_send,
    farpart_recv,
    farback_send,
    farback_recv,
    send_sem,
    recv_sem,
    load_sem,
):
    r = lax.axis_index("row")
    c = lax.axis_index("col")
    own = (masked_charges, first_image)
    ahead = (next_first, next_second)
    images = (first_image, second_image)
    rows_above = jnp.minimum(REACH, n_rows - 1 - r)
    rows_below = jnp.minimum(REACH, r)
    has_above = r < n_rows - 1
    has_below = r > 0

    def up(o):
        return (lax.rem(r + o, n_rows), c)

    def down(o):
        return (lax.rem(r + n_rows - o, n_rows), c)

    def beside(d):
        return (r, lax.rem(c + d, SLAB))

    def cluster(turn):
        return lax.rem(c + turn, SLAB)

    def ranks(i):
        return pl.ds(pl.multiple_of(i * RANK, RANK), RANK)

    def remote(src, dst, at, device):
        return pltpu.make_async_remote_copy(
            src_ref=src,
            dst_ref=dst,
            send_sem=send_sem.at[at],
            recv_sem=recv_sem.at[at],
            device_id=device,
            device_id_type=MESH,
        )

    def field_copy(a, turn):
        i = cluster(SLAB - turn)
        return remote(own[a].at[i], ahead[a].at[i], a * PER_APPLY + FIELD + turn, down(1))

    def coef_copy(a, o):
        return remote(
            coef_own.at[a, ranks(c), :],
            coef_ahead.at[a, ranks(o - 1), :],
            a * PER_APPLY + COEF + o - 1,
            down(o),
        )

    def ahead_copy(a, turn):
        return remote(
            ahead_send.at[a, turn], ahead_recv.at[a, turn], a * PER_APPLY + AHEAD + turn, up(1)
        )

    def part_copy(a, d):
        return remote(
            part_send.at[a, d - 1], part_recv.at[a, d - 1], a * PER_APPLY + PART + d - 1, beside(d)
        )

    def farpart_copy(a, d):
        return remote(
            farpart_send.at[a, ranks(cluster(d)), :],
            farpart_recv.at[a, d - 1],
            a * PER_APPLY + FARPART + d - 1,
            beside(d),
        )

    def farback_copy(a, o):
        return remote(
            farback_send.at[a, ranks(o - 1), :],
            farback_recv.at[a, o - 1],
            a * PER_APPLY + FARBACK + o - 1,
            up(o),
        )

    def image_copy(a, d):
        return remote(
            images[a].at[c], images[a].at[c], a * PER_APPLY + IMAGE + d - 1, beside(d)
        )

    def dense_copy(d):
        return remote(
            dense_send.at[cluster(d)], dense_recv.at[d - 1], DENSE + d - 1, beside(d)
        )

    def each(count, act):
        def step(o, _):
            act(o)
            return 0

        lax.fori_loop(1, count + 1, step, 0)

    loads = [
        pltpu.make_async_copy(source, target, load_sem.at[at])
        for at, (source, target) in enumerate(
            (
                (charges_hbm, charges),
                (sizes_hbm, sizes_ref),
                (basis_hbm, basis_ref),
                (near_rows_hbm, near_rows_ref),
                (near_cols_hbm, near_cols_ref),
                (near_live_hbm, near_live_ref),
                (far_rows_hbm, far_rows_ref),
                (far_cols_hbm, far_cols_ref),
                (far_live_hbm, far_live_ref),
                (couplings_hbm, couplings),
                (blocks_hbm, blocks),
            )
        )
    ]
    for load in loads:
        load.start()

    coef_ahead[...] = jnp.zeros_like(coef_ahead)
    farback_recv[...] = jnp.zeros_like(farback_recv)

    @pl.when(jnp.logical_not(has_above))
    def _():
        next_first[...] = jnp.zeros_like(next_first)
        next_second[...] = jnp.zeros_like(next_second)

    @pl.when(jnp.logical_not(has_below))
    def _():
        ahead_recv[...] = jnp.zeros_like(ahead_recv)

    barrier = pltpu.get_barrier_semaphore()

    def greet(device):
        pl.semaphore_signal(barrier, inc=1, device_id=device, device_id_type=MESH)

    for d in range(1, SLAB):
        greet(beside(d))
    each(rows_above, lambda o: greet(up(o)))
    each(rows_below, lambda o: greet(down(o)))

    panel = lax.broadcasted_iota(I32, (RHS, PANELS), 1)

    def masked(values, size):
        return jnp.where(panel < size, values, jnp.zeros_like(values))

    def last_of(row, group):
        upto = order_s[row, group]
        before = jnp.where(group > 0, order_s[row, jnp.maximum(group - 1, 0)], 0)
        return jnp.maximum(upto - 1, 0), (upto > before).astype(F32)

    def set_coefficients(a, i):
        coef_own[a, ranks(i), :] = lax.dot_general(
            basis_ref[i], own[a][i], (((1,), (1,)), ((), ())), preferred_element_type=F32
        ).astype(BF16)

    def near_pass(a, order_row, forward, prefix):
        def slot(k, carry):
            total, previous = carry
            key = order_s[order_row, k]
            group = key >> 7
            other = (key >> 4) & 7
            source = own[a][other & 3]
            if forward:
                source = jnp.where(other < SLAB, source, ahead[a][other & 3])
            block = blocks[key & 15]
            product = lax.dot_general(
                source,
                block,
                (((1,), (1 if forward else 0,)), ((), ())),
                preferred_element_type=F32,
            )
            total = total * (group == previous).astype(F32) + product
            prefix[k] = total
            return total, group

        start = (jnp.zeros((RHS, PANELS), F32), jnp.int32(-1))
        lax.fori_loop(0, NEAR, slot, start, unroll=UNROLL)

    for load in loads[0:3]:
        load.wait()
    for i in range(SLAB):
        masked_charges[i] = masked(charges[i], sizes_ref[i])
    set_coefficients(0, c)

    pl.semaphore_wait(barrier, SLAB - 1 + rows_above + rows_below)

    @pl.when(has_below)
    def _():
        for turn in range(SLAB):
            field_copy(0, turn).start()

    each(rows_below, lambda o: coef_copy(0, o).start())

    for load in loads[3:9]:
        load.wait()
    first = r * SLAB
    lane = lax.broadcasted_iota(I32, (1, LANES), 1)
    near_used = near_live_ref[0]
    by_row = jnp.broadcast_to((1 << 16) + lane, (1, LANES))
    by_col = by_row
    for s in range(NEAR):
        row = jnp.clip(near_rows_ref[s] - first, 0, SLAB - 1)
        col = jnp.clip(near_cols_ref[s] - first, 0, 2 * SLAB - 1)
        used = s < near_used
        row_key = (jnp.where(used, row, SLAB) << 7) + (col << 4) + s
        col_key = (jnp.where(used, col, 2 * SLAB) << 7) + (row << 4) + s
        by_row = jnp.where(lane == s, row_key, by_row)
        by_col = jnp.where(lane == s, col_key, by_col)
    for at, keys in enumerate((by_row, by_col)):
        ordered, laid = sort_keys(keys)
        order_v[2 * at : 2 * at + 1, :] = ordered
        order_v[2 * at + 1 : 2 * at + 2, :] = count_upto(laid, 7)
    order_v[4:8, :] = jnp.zeros((4, LANES), I32)
    share_order = pltpu.make_async_copy(order_v, order_s, load_sem.at[11])
    share_order.start()

    far_row = jnp.clip(far_rows_ref[...] - first, 0, SLAB - 1).reshape(1, LANES)
    far_col = jnp.clip(far_cols_ref[...] - first - SLAB, 0, REACH * SLAB - 1).reshape(1, LANES)
    far_slab = far_col >> 2
    far_key = (far_col & 3) * (2 * SLAB) + far_row
    far_key = jnp.where(lane < far_live_ref[0], far_key, -2 * SLAB)
    loads[9].wait()
    target = lax.broadcasted_iota(I32, (8 * SLAB, 2 * LANES), 0)
    chosen = jnp.where(target == jnp.concatenate([far_key, far_key + SLAB], axis=1), 1.0, 0.0)
    chosen = chosen.astype(BF16)
    in_slab = [
        jnp.broadcast_to(jnp.where(far_slab == o, 1.0, 0.0), (RANK, LANES)).astype(BF16)
        for o in range(REACH)
    ]

    def dense_rows(m, _):
        halves = []
        for half in range(2):
            block = couplings[2 * m + half]
            tiles = [block * in_slab[o] for o in range(REACH)] + [jnp.zeros_like(block)]
            halves.append(jnp.concatenate(tiles, axis=0))
        rows = lax.dot_general(
            chosen,
            jnp.concatenate(halves, axis=1),
            (((1,), (1,)), ((), ())),
            preferred_element_type=F32,
        )
        for i in range(SLAB):
            dense_sum[i, pl.ds(pl.multiple_of(8 * m, 8), 8), :] = rows[8 * i : 8 * i + 8]
        return 0

    lax.fori_loop(0, RANK // 2, dense_rows, 0, unroll=4)
    for d in TURNS[:3]:
        i = cluster(d)
        dense_send[i] = dense_sum[i].astype(BF16)
        dense_copy(d).start()
    for i in range(SLAB):

        @pl.when(i != c)
        def _():
            set_coefficients(0, i)

    share_order.wait()
    loads[10].wait()

    for a in range(2):
        near_pass(a, 2, False, back_prefix)

        @pl.when(has_above)
        def _():
            for turn in TURNS:
                at, live = last_of(3, SLAB + cluster(turn))
                ahead_send[a, turn] = (back_prefix[at] * live).astype(BF16)
                ahead_copy(a, turn).start()

        def far_back():
            farback_send[a] = lax.dot_general(
                dense[...], coef_own[a], (((0,), (0,)), ((), ())), preferred_element_type=F32
            ).astype(BF16)
            each(rows_above, lambda o: farback_copy(a, o).start())

        if a == 1:
            far_back()

        @pl.when(has_above)
        def _():
            for turn in range(SLAB):
                field_copy(a, turn).wait_recv()

        near_pass(a, 0, True, near_prefix)

        if a == 0:
            for d in TURNS[:3]:
                dense_copy(d).wait_recv()
            total = dense_sum[c]
            for d in range(SLAB - 1):
                total = total + dense_recv[d].astype(F32)
            at = lax.broadcasted_iota(I32, (LANES, LANES), 0)
            wanted = (at & (RANK - 1)) * SLAB + (at >> 5)
            move = jnp.where(lax.broadcasted_iota(I32, (LANES, LANES), 1) == wanted, 1.0, 0.0)
            dense[...] = jnp.dot(
                move.astype(BF16), total.astype(BF16), preferred_element_type=F32
            ).astype(BF16)
            far_back()

        for turn in TURNS:
            i = cluster(turn)

            @pl.when(has_below)
            def _():
                ahead_copy(a, turn).wait_recv()

            at, live = last_of(1, i)
            image = near_prefix[at] * live
            at, live = last_of(3, i)
            image = image + back_prefix[at] * live + ahead_recv[a, turn].astype(F32)
            if turn > 0:
                part_send[a, turn - 1] = image.astype(BF16)
                part_copy(a, turn).start()

        each(rows_above, lambda o: coef_copy(a, o).wait_recv())
        farpart_send[a] = jnp.dot(
            dense[...], coef_ahead[a], preferred_element_type=F32
        ).astype(BF16)
        for d in TURNS[:3]:
            farpart_copy(a, d).start()
        far_total = farpart_send[a, ranks(c), :].astype(F32)

        each(rows_below, lambda o: farback_copy(a, o).wait_recv())
        for o in range(REACH):
            far_total = far_total + farback_recv[a, o].astype(F32)
        for d in TURNS[:3]:
            part_copy(a, d).wait_recv()
            image = image + part_recv[a, d - 1].astype(F32)
        for d in TURNS[:3]:
            farpart_copy(a, d).wait_recv()
            far_total = far_total + farpart_recv[a, d - 1].astype(F32)
        image = image + lax.dot_general(
            far_total.astype(BF16),
            basis_ref[c],
            (((0,), (0,)), ((), ())),
            preferred_element_type=F32,
        )
        images[a][c] = masked(image, sizes_ref[c]).astype(BF16)
        for d in TURNS[:3]:
            image_copy(a, d).start()
        if a == 0:

            @pl.when(has_below)
            def _():
                field_copy(1, 0).start()

            set_coefficients(1, c)
            each(rows_below, lambda o: coef_copy(1, o).start())
        for d in (1, 3, 2):
            image_copy(a, d).wait_recv()
            if a == 0:

                @pl.when(has_below)
                def _():
                    field_copy(1, d).start()

        if a == 0:
            for d in (1, 3, 2):
                set_coefficients(1, cluster(SLAB - d))

    for a in range(2):
        for d in range(1, SLAB):
            part_copy(a, d).wait_send()
            farpart_copy(a, d).wait_send()
            image_copy(a, d).wait_send()
        each(rows_below, lambda o: coef_copy(a, o).wait_send())
        each(rows_above, lambda o: farback_copy(a, o).wait_send())

        @pl.when(has_below)
        def _():
            for turn in range(SLAB):
                field_copy(a, turn).wait_send()

        @pl.when(has_above)
        def _():
            for turn in range(SLAB):
                ahead_copy(a, turn).wait_send()

    for d in range(1, SLAB):
        dense_copy(d).wait_send()


def per_device(n_rows, *arrays):
    arrays = list(arrays)
    arrays[7] = jnp.transpose(arrays[7], (1, 2, 0))
    for n in range(11):
        if arrays[n].size > 1:
            arrays[n] = pltpu.with_memory_space_constraint(arrays[n], pltpu.HBM)
    hbm = pl.BlockSpec(memory_space=pltpu.HBM)
    vmem = pl.BlockSpec(memory_space=pltpu.VMEM)
    image = jax.ShapeDtypeStruct((SLAB, RHS, PANELS), BF16)
    return pl.pallas_call(
        functools.partial(kernel, n_rows),
        out_shape=(image, image),
        in_specs=[hbm] * 11,
        out_specs=(vmem, vmem),
        scratch_shapes=[
            pltpu.VMEM((SLAB, RHS, PANELS), BF16),
            pltpu.VMEM((SLAB, RANK, PANELS), BF16),
            pltpu.SMEM((SLAB,), I32),
            pltpu.VMEM((NEAR, PANELS, PANELS), BF16),
            pltpu.SMEM((NEAR,), I32),
            pltpu.SMEM((NEAR,), I32),
            pltpu.SMEM((1,), I32),
            pltpu.VMEM((RANK, RANK, FAR), BF16),
            pltpu.VMEM((FAR,), I32),
            pltpu.VMEM((FAR,), I32),
            pltpu.SMEM((1,), I32),
            pltpu.VMEM((SLAB, RHS, PANELS), BF16),
            pltpu.VMEM((SLAB, RHS, PANELS), BF16),
            pltpu.VMEM((SLAB, RHS, PANELS), BF16),
            pltpu.VMEM((8, LANES), I32),
            pltpu.SMEM((8, LANES), I32),
            pltpu.VMEM((2, SLAB * RANK, RHS), BF16),
            pltpu.VMEM((2, (REACH + 1) * RANK, RHS), BF16),
            pltpu.VMEM((SLAB, SLAB * RANK, 2 * LANES), F32),
            pltpu.VMEM((SLAB, SLAB * RANK, 2 * LANES), BF16),
            pltpu.VMEM((SLAB - 1, SLAB * RANK, 2 * LANES), BF16),
            pltpu.VMEM((SLAB * RANK, 2 * LANES), BF16),
            pltpu.VMEM((NEAR, RHS, PANELS), F32),
            pltpu.VMEM((NEAR, RHS, PANELS), F32),
            pltpu.VMEM((2, SLAB, RHS, PANELS), BF16),
            pltpu.VMEM((2, SLAB, RHS, PANELS), BF16),
            pltpu.VMEM((2, SLAB - 1, RHS, PANELS), BF16),
            pltpu.VMEM((2, SLAB - 1, RHS, PANELS), BF16),
            pltpu.VMEM((2, SLAB * RANK, RHS), BF16),
            pltpu.VMEM((2, SLAB - 1, RANK, RHS), BF16),
            pltpu.VMEM((2, (REACH + 1) * RANK, RHS), BF16),
            pltpu.VMEM((2, REACH, RANK, RHS), BF16),
            pltpu.SemaphoreType.DMA((N_SEMS,)),
            pltpu.SemaphoreType.DMA((N_SEMS,)),
            pltpu.SemaphoreType.DMA((12,)),
        ],
        compiler_params=pltpu.CompilerParams(
            collective_id=0, has_side_effects=True, vmem_limit_bytes=40 * 1024 * 1024
        ),
    )(*arrays)


def solution(mesh):
    placed = (
        P("row", None, None),
        P("row", None, None),
        P("row"),
        P(("row", "col"), None, None),
        P(("row", "col")),
        P(("row", "col")),
        P(("row", "col")),
        P(("row", "col"), None, None),
        P(("row", "col")),
        P(("row", "col")),
        P(("row", "col")),
    )
    return jax.shard_map(
        functools.partial(per_device, mesh.shape["row"]),
        mesh=mesh,
        in_specs=placed,
        out_specs=(P("row", None, None), P("row", None, None)),
        check_vma=False,
    )
```

```python
import functools

import jax
import jax.numpy as jnp
from jax import lax
from jax.experimental import pallas as pl
from jax.experimental.pallas import tpu as pltpu
from jax.sharding import PartitionSpec as P

MESH = pl.DeviceIdType.MESH
F32 = jnp.float32
BF16 = jnp.bfloat16
I32 = jnp.int32

SLAB = 4
REACH = 7
TILES = 4
NEAR = 16
FAR = 128
RANK = 32
RHS = 128
PANELS = 256
LANES = 128
HALF = RHS // 2
UNROLL = 8

FIELD, AHEAD, PART, IMAGE, COEF, FARBACK, FARPART, SIBLING, PER_APPLY = 0, 8, 16, 22, 28, 32, 36, 43, 44
DENSE = 2 * PER_APPLY
N_SEMS = DENSE + 7
TURNS = (2, 1, 3, 0)


def sort_keys(unique_keys):
    across = jnp.broadcast_to(unique_keys, (LANES, LANES))
    down = across.T
    rank = jnp.sum(jnp.where(across < down, 1, 0).astype(I32), axis=1, keepdims=True)
    lane = lax.broadcasted_iota(I32, (LANES, LANES), 1)
    ordered = jnp.sum(jnp.where(rank == lane, down, 0), axis=0, keepdims=True)
    return ordered, down


def count_upto(down, shift):
    lane = lax.broadcasted_iota(I32, (LANES, LANES), 1)
    return jnp.sum(jnp.where((down >> shift) <= lane, 1, 0).astype(I32), axis=0, keepdims=True)


def kernel(
    n_rows,
    charges_hbm,
    basis_hbm,
    sizes_hbm,
    blocks_hbm,
    near_rows_hbm,
    near_cols_hbm,
    near_live_hbm,
    couplings_hbm,
    far_rows_hbm,
    far_cols_hbm,
    far_live_hbm,
    first_image,
    second_image,
    charges,
    basis_ref,
    sizes_ref,
    blocks,
    near_rows_ref,
    near_cols_ref,
    near_live_ref,
    couplings,
    far_rows_ref,
    far_cols_ref,
    far_live_ref,
    masked_low,
    masked_high,
    own_low,
    own_high,
    next_first_low,
    next_first_high,
    next_second_low,
    next_second_high,
    order_v,
    order_s,
    coef_own,
    coef_sibling,
    coef_ahead,
    dense_sum,
    dense_send,
    dense_recv,
    dense,
    near_prefix,
    back_prefix,
    ahead_send,
    ahead_recv,
    part_send,
    part_recv,
    farpart_send,
    farpart_recv,
    farback_send,
    farback_recv,
    send_sem,
    recv_sem,
    load_sem,
):
    r = lax.axis_index("row")
    c = lax.axis_index("col")
    own = ((masked_low, masked_high), (own_low, own_high))
    ahead = ((next_first_low, next_first_high), (next_second_low, next_second_high))
    halves = (slice(0, HALF), slice(HALF, RHS))
    odd = lax.rem(r, 2)
    sibling = r + 1 - 2 * odd
    rows_above = jnp.minimum(TILES - odd, (n_rows - 1 - r) // 2)
    rows_below = jnp.minimum(TILES - odd, r // 2)
    has_above = r < n_rows - 1
    has_below = r > 0

    def up(o):
        return (lax.rem(r + o, n_rows), c)

    def down(o):
        return (lax.rem(r + n_rows - o, n_rows), c)

    def beside(d):
        return (r, lax.rem(c + d, SLAB))

    def across(d):
        return (sibling, lax.rem(c + d, SLAB))

    def cluster(turn):
        return lax.rem(c + turn, SLAB)

    def ranks(i):
        return pl.ds(pl.multiple_of(i * RANK, RANK), RANK)

    def remote(src, dst, at, device):
        return pltpu.make_async_remote_copy(
            src_ref=src,
            dst_ref=dst,
            send_sem=send_sem.at[at],
            recv_sem=recv_sem.at[at],
            device_id=device,
            device_id_type=MESH,
        )

    def field_copy(a, turn, h):
        i = cluster(SLAB - turn)
        at = a * PER_APPLY + FIELD + SLAB * h + turn
        return remote(own[a][h].at[i], ahead[a][h].at[i], at, down(1))

    def coef_copy(a, m):
        return remote(
            coef_own.at[a, ranks(c), :],
            coef_ahead.at[a, ranks(m - 1 + odd), :],
            a * PER_APPLY + COEF + m - 1,
            down(2 * m),
        )

    def sibling_copy(a):
        return remote(
            coef_own.at[a], coef_sibling.at[a], a * PER_APPLY + SIBLING, across(0)
        )

    def ahead_copy(a, turn, h):
        return remote(
            ahead_send.at[a, turn, halves[h], :],
            ahead_recv.at[a, turn, halves[h], :],
            a * PER_APPLY + AHEAD + SLAB * h + turn,
            up(1),
        )

    def part_copy(a, d, h):
        return remote(
            part_send.at[a, d - 1, halves[h], :],
            part_recv.at[a, d - 1, halves[h], :],
            a * PER_APPLY + PART + (SLAB - 1) * h + d - 1,
            beside(d),
        )

    def farpart_copy(a, d):
        return remote(
            farpart_send.at[a, ranks(cluster(d)), :],
            farpart_recv.at[a, d - 1],
            a * PER_APPLY + FARPART + d - 1,
            beside(d),
        )

    def farcross_copy(a, d):
        return remote(
            farpart_send.at[a, ranks(SLAB + cluster(d)), :],
            farpart_recv.at[a, SLAB - 1 + d],
            a * PER_APPLY + FARPART + SLAB - 1 + d,
            across(d),
        )

    def farback_copy(a, m):
        return remote(
            farback_send.at[a, ranks(m - 1 + odd), :],
            farback_recv.at[a, m - 1],
            a * PER_APPLY + FARBACK + m - 1,
            up(2 * m),
        )

    def image_copy(a, d, h):
        mine = own[1][h].at[c] if a == 0 else second_image.at[c, halves[h], :]
        return remote(mine, mine, a * PER_APPLY + IMAGE + (SLAB - 1) * h + d - 1, beside(d))

    def dense_copy(d):
        return remote(
            dense_send.at[1, cluster(d)], dense_recv.at[d - 1], DENSE + d - 1, beside(d)
        )

    def dense_cross_copy(d):
        return remote(
            dense_send.at[0, cluster(d)],
            dense_recv.at[SLAB - 1 + d],
            DENSE + SLAB - 1 + d,
            across(d),
        )

    def each(count, act):
        def step(o, _):
            act(o)
            return 0

        lax.fori_loop(1, count + 1, step, 0)

    loads = [
        pltpu.make_async_copy(source, target, load_sem.at[at])
        for at, (source, target) in enumerate(
            (
                (charges_hbm, charges),
                (sizes_hbm, sizes_ref),
                (basis_hbm, basis_ref),
                (near_rows_hbm, near_rows_ref),
                (near_cols_hbm, near_cols_ref),
                (near_live_hbm, near_live_ref),
                (far_rows_hbm, far_rows_ref),
                (far_cols_hbm, far_cols_ref),
                (far_live_hbm, far_live_ref),
                (couplings_hbm, couplings),
                (blocks_hbm, blocks),
            )
        )
    ]
    for load in loads:
        load.start()

    coef_ahead[...] = jnp.zeros_like(coef_ahead)
    farback_recv[...] = jnp.zeros_like(farback_recv)

    @pl.when(jnp.logical_not(has_above))
    def _():
        for a in range(2):
            for h in range(2):
                ahead[a][h][...] = jnp.zeros_like(ahead[a][h])

    @pl.when(jnp.logical_not(has_below))
    def _():
        ahead_recv[...] = jnp.zeros_like(ahead_recv)

    barrier = pltpu.get_barrier_semaphore()

    def greet(device):
        pl.semaphore_signal(barrier, inc=1, device_id=device, device_id_type=MESH)

    for d in range(1, SLAB):
        greet(beside(d))
    for d in range(SLAB):
        greet(across(d))
    each(rows_above, lambda m: greet(up(2 * m)))
    each(rows_below, lambda m: greet(down(2 * m)))
    has_outer = jnp.where(odd == 1, r < n_rows - 1, r > 0)

    @pl.when(has_outer)
    def _():
        greet(up(jnp.where(odd == 1, 1, n_rows - 1)))


    def masked(values, size):
        panel = lax.broadcasted_iota(I32, values.shape, 1)
        return jnp.where(panel < size, values, jnp.zeros_like(values))

    def last_of(row, group):
        upto = order_s[row, group]
        before = jnp.where(group > 0, order_s[row, jnp.maximum(group - 1, 0)], 0)
        return jnp.maximum(upto - 1, 0), (upto > before).astype(F32)

    def set_coefficients(a, i):
        coef_own[a, ranks(i), :] = lax.dot_general(
            basis_ref[i],
            jnp.concatenate([own[a][0][i], own[a][1][i]], axis=0),
            (((1,), (1,)), ((), ())),
            preferred_element_type=F32,
        ).astype(BF16)

    def near_pass(a, order_row, forward, prefix, h):
        def slot(k, carry):
            total, previous = carry
            key = order_s[order_row, k]
            group = key >> 7
            other = (key >> 4) & 7
            source = own[a][h][other & 3]
            if forward:
                source = jnp.where(other < SLAB, source, ahead[a][h][other & 3])
            block = blocks[key & 15]
            product = lax.dot_general(
                source,
                block,
                (((1,), (1 if forward else 0,)), ((), ())),
                preferred_element_type=F32,
            )
            total = total * (group == previous).astype(F32) + product
            prefix[h, k] = total
            return total, group

        start = (jnp.zeros((HALF, PANELS), F32), jnp.int32(-1))
        lax.fori_loop(0, NEAR, slot, start, unroll=UNROLL)

    for load in loads[0:3]:
        load.wait()
    for i in range(SLAB):
        values = masked(charges[i], sizes_ref[i])
        for h in range(2):
            own[0][h][i] = values[halves[h]]
    set_coefficients(0, c)

    first = r * SLAB
    lane = lax.broadcasted_iota(I32, (1, LANES), 1)
    for load in loads[3:6]:
        load.wait()
    near_used = near_live_ref[0]
    by_row = jnp.broadcast_to((1 << 16) + lane, (1, LANES))
    by_col = by_row
    for s in range(NEAR):
        row = jnp.clip(near_rows_ref[s] - first, 0, SLAB - 1)
        col = jnp.clip(near_cols_ref[s] - first, 0, 2 * SLAB - 1)
        used = s < near_used
        row_key = (jnp.where(used, row, SLAB) << 7) + (col << 4) + s
        col_key = (jnp.where(used, col, 2 * SLAB) << 7) + (row << 4) + s
        by_row = jnp.where(lane == s, row_key, by_row)
        by_col = jnp.where(lane == s, col_key, by_col)
    for at, keys in enumerate((by_row, by_col)):
        ordered, laid = sort_keys(keys)
        order_v[2 * at : 2 * at + 1, :] = ordered
        order_v[2 * at + 1 : 2 * at + 2, :] = count_upto(laid, 7)
    order_v[4:8, :] = jnp.zeros((4, LANES), I32)
    share_order = pltpu.make_async_copy(order_v, order_s, load_sem.at[11])
    share_order.start()

    for load in loads[6:9]:
        load.wait()
    far_row = jnp.clip(far_rows_ref[...] - first, 0, SLAB - 1).reshape(1, LANES)
    far_col = jnp.clip(far_cols_ref[...] - first - SLAB, 0, REACH * SLAB - 1).reshape(1, LANES)
    far_slab = far_col >> 2
    far_tile = (far_slab >> 1) + jnp.where((far_slab & 1) == 1, TILES + odd, 0)
    far_key = (far_col & 3) * (2 * SLAB) + far_row
    far_key = jnp.where(lane < far_live_ref[0], far_key, -2 * SLAB)
    loads[9].wait()
    target = lax.broadcasted_iota(I32, (8 * SLAB, 2 * LANES), 0)
    chosen = jnp.where(target == jnp.concatenate([far_key, far_key + SLAB], axis=1), 1.0, 0.0)
    chosen = chosen.astype(BF16)
    in_slab = [
        jnp.broadcast_to(jnp.where(far_tile == o, 1.0, 0.0), (RANK, LANES)).astype(BF16)
        for o in range(2 * TILES)
    ]

    def dense_rows(m, _):
        halves = []
        for half in range(2):
            block = couplings[2 * m + half]
            tiles = [block * in_slab[o] for o in range(2 * TILES)]
            halves.append(jnp.concatenate(tiles, axis=0))
        rows = lax.dot_general(
            chosen,
            jnp.concatenate(halves, axis=1),
            (((1,), (1,)), ((), ())),
            preferred_element_type=F32,
        )
        for i in range(SLAB):
            dense_sum[i, pl.ds(pl.multiple_of(8 * m, 8), 8), :] = rows[8 * i : 8 * i + 8]
        return 0

    lax.fori_loop(0, RANK // 2, dense_rows, 0, unroll=4)
    pl.semaphore_wait(
        barrier, 2 * SLAB - 1 + rows_above + rows_below + jnp.where(has_outer, 1, 0)
    )

    @pl.when(has_below)
    def _():
        for h in range(2):
            for turn in range(SLAB):
                field_copy(0, turn, h).start()

    for d in TURNS:
        i = cluster(d)
        dense_send[0, i] = dense_sum[i][:, :LANES].astype(BF16)
        dense_cross_copy(d).start()
        if d > 0:
            dense_send[1, i] = dense_sum[i][:, LANES:].astype(BF16)
            dense_copy(d).start()
    each(rows_below, lambda m: coef_copy(0, m).start())

    for i in range(SLAB):

        @pl.when(i != c)
        def _():
            set_coefficients(0, i)

    sibling_copy(0).start()

    def own_tile(a):
        @pl.when(odd == 1)
        def _():
            coef_ahead[a, 0:RANK, :] = coef_own[a, ranks(c), :]

    own_tile(0)
    share_order.wait()
    loads[10].wait()

    for a in range(2):
        for h in range(2):
            if a == 1:
                for d in (1, 3, 2):
                    image_copy(0, d, h).wait_recv()

                    @pl.when(has_below)
                    def _():
                        field_copy(1, d, h).start()

            near_pass(a, 2, False, back_prefix, h)

            @pl.when(has_above)
            def _():
                for turn in TURNS:
                    at, live = last_of(3, SLAB + cluster(turn))
                    ahead_send[a, turn, halves[h], :] = (back_prefix[h, at] * live).astype(BF16)
                    ahead_copy(a, turn, h).start()

        def far_back():
            sibling_copy(a).wait_recv()
            both = jnp.concatenate([coef_own[a], coef_sibling[a]], axis=0)
            farback_send[a] = lax.dot_general(
                dense[...], both, (((0,), (0,)), ((), ())), preferred_element_type=F32
            ).astype(BF16)
            each(rows_above, lambda m: farback_copy(a, m).start())

        if a == 1:
            for d in (1, 3, 2):
                set_coefficients(1, cluster(SLAB - d))
            sibling_copy(1).start()

        own_parts = []
        for h in range(2):
            @pl.when(has_above)
            def _():
                for turn in range(SLAB):
                    field_copy(a, turn, h).wait_recv()

            near_pass(a, 0, True, near_prefix, h)

            for turn in TURNS:
                i = cluster(turn)

                @pl.when(has_below)
                def _():
                    ahead_copy(a, turn, h).wait_recv()

                at, live = last_of(1, i)
                image = near_prefix[h, at] * live
                at, live = last_of(3, i)
                image = image + back_prefix[h, at] * live
                image = image + ahead_recv[a, turn, halves[h], :].astype(F32)
                if turn > 0:
                    part_send[a, turn - 1, halves[h], :] = image.astype(BF16)
                    part_copy(a, turn, h).start()
            own_parts.append(image)

            if h == 0:
                if a == 0:
                    for d in TURNS:
                        dense_cross_copy(d).wait_recv()
                        if d > 0:
                            dense_copy(d).wait_recv()
                    at = lax.broadcasted_iota(I32, (LANES, LANES), 0)
                    wanted = (at & (RANK - 1)) * SLAB + (at >> 5)
                    move = jnp.where(lax.broadcasted_iota(I32, (LANES, LANES), 1) == wanted, 1.0, 0.0)
                    move = move.astype(BF16)
                    total = dense_sum[c][:, LANES:]
                    for d in range(SLAB - 1):
                        total = total + dense_recv[d].astype(F32)
                    dense[0:LANES, :] = jnp.dot(
                        move, total.astype(BF16), preferred_element_type=F32
                    ).astype(BF16)
                    total = dense_recv[SLAB - 1].astype(F32)
                    for d in range(1, SLAB):
                        total = total + dense_recv[SLAB - 1 + d].astype(F32)
                    dense[LANES:, :] = jnp.dot(
                        move, total.astype(BF16), preferred_element_type=F32
                    ).astype(BF16)
                far_back()

                each(rows_above, lambda m: coef_copy(a, m).wait_recv())
                farpart_send[a] = jnp.dot(
                    dense[...], coef_ahead[a], preferred_element_type=F32
                ).astype(BF16)
                for d in TURNS:
                    farcross_copy(a, d).start()
                    if d > 0:
                        farpart_copy(a, d).start()
        far_total = farpart_send[a, ranks(c), :].astype(F32)
        far_total = far_total + jnp.where(odd == 1, farback_send[a, 0:RANK, :], 0).astype(F32)

        each(rows_below, lambda m: farback_copy(a, m).wait_recv())
        for m in range(TILES):
            far_total = far_total + farback_recv[a, m].astype(F32)
        for d in TURNS:
            farcross_copy(a, d).wait_recv()
            if d > 0:
                farpart_copy(a, d).wait_recv()
        for d in range(2 * SLAB - 1):
            far_total = far_total + farpart_recv[a, d].astype(F32)
        far_image = lax.dot_general(
            far_total.astype(BF16),
            basis_ref[c],
            (((0,), (0,)), ((), ())),
            preferred_element_type=F32,
        )
        for h in range(2):
            image = own_parts[h] + far_image[halves[h]]
            for d in TURNS[:3]:
                part_copy(a, d, h).wait_recv()
                image = image + part_recv[a, d - 1, halves[h], :].astype(F32)
            image = masked(image, sizes_ref[c]).astype(BF16)
            if a == 0:
                own[1][h][c] = image
            else:
                second_image[c, halves[h], :] = image
            for d in TURNS[:3]:
                image_copy(a, d, h).start()
            if a == 0:

                @pl.when(has_below)
                def _():
                    field_copy(1, 0, h).start()

        if a == 0:
            set_coefficients(1, c)
            each(rows_below, lambda m: coef_copy(1, m).start())
            own_tile(1)

    for h in range(2):
        first_image[:, halves[h], :] = own[1][h][...]
        for d in (1, 3, 2):
            image_copy(1, d, h).wait_recv()

    for a in range(2):
        for d in range(1, SLAB):
            farpart_copy(a, d).wait_send()
            for h in range(2):
                part_copy(a, d, h).wait_send()
                image_copy(a, d, h).wait_send()
        for d in range(SLAB):
            farcross_copy(a, d).wait_send()
        sibling_copy(a).wait_send()
        each(rows_below, lambda m: coef_copy(a, m).wait_send())
        each(rows_above, lambda m: farback_copy(a, m).wait_send())

        @pl.when(has_below)
        def _():
            for turn in range(SLAB):
                for h in range(2):
                    field_copy(a, turn, h).wait_send()

        @pl.when(has_above)
        def _():
            for turn in range(SLAB):
                for h in range(2):
                    ahead_copy(a, turn, h).wait_send()

    for d in range(1, SLAB):
        dense_copy(d).wait_send()
    for d in range(SLAB):
        dense_cross_copy(d).wait_send()


def per_device(n_rows, *arrays):
    arrays = list(arrays)
    arrays[7] = jnp.transpose(arrays[7], (1, 2, 0))
    for n in range(11):
        if arrays[n].size > 1:
            arrays[n] = pltpu.with_memory_space_constraint(arrays[n], pltpu.HBM)
    hbm = pl.BlockSpec(memory_space=pltpu.HBM)
    vmem = pl.BlockSpec(memory_space=pltpu.VMEM)
    image = jax.ShapeDtypeStruct((SLAB, RHS, PANELS), BF16)
    return pl.pallas_call(
        functools.partial(kernel, n_rows),
        out_shape=(image, image),
        in_specs=[hbm] * 11,
        out_specs=(vmem, vmem),
        scratch_shapes=[
            pltpu.VMEM((SLAB, RHS, PANELS), BF16),
            pltpu.VMEM((SLAB, RANK, PANELS), BF16),
            pltpu.SMEM((SLAB,), I32),
            pltpu.VMEM((NEAR, PANELS, PANELS), BF16),
            pltpu.SMEM((NEAR,), I32),
            pltpu.SMEM((NEAR,), I32),
            pltpu.SMEM((1,), I32),
            pltpu.VMEM((RANK, RANK, FAR), BF16),
            pltpu.VMEM((FAR,), I32),
            pltpu.VMEM((FAR,), I32),
            pltpu.SMEM((1,), I32),
            pltpu.VMEM((SLAB, HALF, PANELS), BF16),
            pltpu.VMEM((SLAB, HALF, PANELS), BF16),
            pltpu.VMEM((SLAB, HALF, PANELS), BF16),
            pltpu.VMEM((SLAB, HALF, PANELS), BF16),
            pltpu.VMEM((SLAB, HALF, PANELS), BF16),
            pltpu.VMEM((SLAB, HALF, PANELS), BF16),
            pltpu.VMEM((SLAB, HALF, PANELS), BF16),
            pltpu.VMEM((SLAB, HALF, PANELS), BF16),
            pltpu.VMEM((8, LANES), I32),
            pltpu.SMEM((8, LANES), I32),
            pltpu.VMEM((2, SLAB * RANK, RHS), BF16),
            pltpu.VMEM((2, SLAB * RANK, RHS), BF16),
            pltpu.VMEM((2, TILES * RANK, RHS), BF16),
            pltpu.VMEM((SLAB, SLAB * RANK, 2 * LANES), F32),
            pltpu.VMEM((2, SLAB, SLAB * RANK, LANES), BF16),
            pltpu.VMEM((2 * SLAB - 1, SLAB * RANK, LANES), BF16),
            pltpu.VMEM((2 * SLAB * RANK, LANES), BF16),
            pltpu.VMEM((2, NEAR, HALF, PANELS), F32),
            pltpu.VMEM((2, NEAR, HALF, PANELS), F32),
            pltpu.VMEM((2, SLAB, RHS, PANELS), BF16),
            pltpu.VMEM((2, SLAB, RHS, PANELS), BF16),
            pltpu.VMEM((2, SLAB - 1, RHS, PANELS), BF16),
            pltpu.VMEM((2, SLAB - 1, RHS, PANELS), BF16),
            pltpu.VMEM((2, 2 * SLAB * RANK, RHS), BF16),
            pltpu.VMEM((2, 2 * SLAB - 1, RANK, RHS), BF16),
            pltpu.VMEM((2, TILES * RANK, RHS), BF16),
            pltpu.VMEM((2, TILES, RANK, RHS), BF16),
            pltpu.SemaphoreType.DMA((N_SEMS,)),
            pltpu.SemaphoreType.DMA((N_SEMS,)),
            pltpu.SemaphoreType.DMA((12,)),
        ],
        compiler_params=pltpu.CompilerParams(
            collective_id=0, has_side_effects=True, vmem_limit_bytes=40 * 1024 * 1024
        ),
    )(*arrays)


def solution(mesh):
    placed = (
        P("row", None, None),
        P("row", None, None),
        P("row"),
        P(("row", "col"), None, None),
        P(("row", "col")),
        P(("row", "col")),
        P(("row", "col")),
        P(("row", "col"), None, None),
        P(("row", "col")),
        P(("row", "col")),
        P(("row", "col")),
    )
    return jax.shard_map(
        functools.partial(per_device, mesh.shape["row"]),
        mesh=mesh,
        in_specs=placed,
        out_specs=(P("row", None, None), P("row", None, None)),
        check_vma=False,
    )
```

```python
import functools

import jax
import jax.numpy as jnp
from jax import lax
from jax.experimental import pallas as pl
from jax.experimental.pallas import tpu as pltpu
from jax.sharding import PartitionSpec as P

MESH = pl.DeviceIdType.MESH
F32 = jnp.float32
BF16 = jnp.bfloat16
I32 = jnp.int32

SLAB = 4
REACH = 7
TILES = 4
NEAR = 16
FAR = 128
RANK = 32
RHS = 128
PANELS = 256
LANES = 128
HALF = RHS // 2
UNROLL = 8
BACK_AT, PART_AT = (1, -1), (1, 0)

FIELD, AHEAD, PART, IMAGE, COEF, FARBACK, FARPART, SHARE, PER_APPLY = 0, 8, 16, 22, 28, 32, 36, 43, 50
DENSE = 2 * PER_APPLY
N_SEMS = DENSE + 7
TURNS = (2, 1, 3, 0)


def sort_keys(unique_keys):
    across = jnp.broadcast_to(unique_keys, (LANES, LANES))
    down = across.T
    rank = jnp.sum(jnp.where(across < down, 1, 0).astype(I32), axis=1, keepdims=True)
    lane = lax.broadcasted_iota(I32, (LANES, LANES), 1)
    ordered = jnp.sum(jnp.where(rank == lane, down, 0), axis=0, keepdims=True)
    return ordered, down


def count_upto(down, shift):
    lane = lax.broadcasted_iota(I32, (LANES, LANES), 1)
    return jnp.sum(jnp.where((down >> shift) <= lane, 1, 0).astype(I32), axis=0, keepdims=True)


def kernel(
    n_rows,
    charges_hbm,
    basis_hbm,
    sizes_hbm,
    blocks_hbm,
    near_rows_hbm,
    near_cols_hbm,
    near_live_hbm,
    couplings_hbm,
    far_rows_hbm,
    far_cols_hbm,
    far_live_hbm,
    first_image,
    second_image,
    charges,
    basis_ref,
    sizes_ref,
    blocks,
    near_rows_ref,
    near_cols_ref,
    near_live_ref,
    couplings,
    far_rows_ref,
    far_cols_ref,
    far_live_ref,
    masked_low,
    masked_high,
    own_low,
    own_high,
    next_first_low,
    next_first_high,
    next_second_low,
    next_second_high,
    order_v,
    order_s,
    coef_own,
    coef_sibling,
    coef_ahead,
    dense_sum,
    dense_send,
    dense_recv,
    dense,
    near_prefix,
    back_prefix,
    ahead_send,
    ahead_recv,
    part_send,
    part_recv,
    farpart_send,
    farpart_recv,
    farback_send,
    farback_recv,
    send_sem,
    recv_sem,
    load_sem,
):
    r = lax.axis_index("row")
    c = lax.axis_index("col")
    own = ((masked_low, masked_high), (own_low, own_high))
    ahead = ((next_first_low, next_first_high), (next_second_low, next_second_high))
    halves = (slice(0, HALF), slice(HALF, RHS))
    odd = lax.rem(r, 2)
    sibling = r + 1 - 2 * odd
    rows_above = jnp.minimum(TILES - odd, (n_rows - 1 - r) // 2)
    rows_below = jnp.minimum(TILES - odd, r // 2)
    has_above = r < n_rows - 1
    has_below = r > 0

    def up(o):
        return (lax.rem(r + o, n_rows), c)

    def down(o):
        return (lax.rem(r + n_rows - o, n_rows), c)

    def beside(d):
        return (r, lax.rem(c + d, SLAB))

    def across(d):
        return (sibling, lax.rem(c + d, SLAB))

    def cluster(turn):
        return lax.rem(c + turn, SLAB)

    def ranks(i):
        return pl.ds(pl.multiple_of(i * RANK, RANK), RANK)

    def remote(src, dst, at, device):
        return pltpu.make_async_remote_copy(
            src_ref=src,
            dst_ref=dst,
            send_sem=send_sem.at[at],
            recv_sem=recv_sem.at[at],
            device_id=device,
            device_id_type=MESH,
        )

    def field_copy(a, turn, h):
        i = cluster(SLAB - turn)
        at = a * PER_APPLY + FIELD + SLAB * h + turn
        return remote(own[a][h].at[i], ahead[a][h].at[i], at, down(1))

    def coef_copy(a, m):
        return remote(
            coef_own.at[a, ranks(c), :],
            coef_ahead.at[a, ranks(m - 1 + odd), :],
            a * PER_APPLY + COEF + m - 1,
            down(2 * m),
        )

    def sibling_copy():
        return remote(coef_own.at[0], coef_sibling.at[0], SHARE, across(0))

    def share_copy(d):
        mine = coef_own.at[1, ranks(c), :]
        return remote(mine, mine, PER_APPLY + SHARE + d - 1, beside(d))

    def share_cross_copy(d):
        return remote(
            coef_own.at[1, ranks(c), :],
            coef_sibling.at[1, ranks(c), :],
            PER_APPLY + SHARE + SLAB - 1 + d,
            across(d),
        )

    def ahead_copy(a, turn, h):
        return remote(
            ahead_send.at[a, turn, halves[h], :],
            ahead_recv.at[a, turn, halves[h], :],
            a * PER_APPLY + AHEAD + SLAB * h + turn,
            up(1),
        )

    def part_copy(a, d, h):
        return remote(
            part_send.at[a, d - 1, halves[h], :],
            part_recv.at[a, d - 1, halves[h], :],
            a * PER_APPLY + PART + (SLAB - 1) * h + d - 1,
            beside(d),
        )

    def farpart_copy(a, d):
        return remote(
            farpart_send.at[a, ranks(cluster(d)), :],
            farpart_recv.at[a, d - 1],
            a * PER_APPLY + FARPART + d - 1,
            beside(d),
        )

    def farcross_copy(a, d):
        return remote(
            farpart_send.at[a, ranks(SLAB + cluster(d)), :],
            farpart_recv.at[a, SLAB - 1 + d],
            a * PER_APPLY + FARPART + SLAB - 1 + d,
            across(d),
        )

    def farback_copy(a, m):
        return remote(
            farback_send.at[a, ranks(m - 1 + odd), :],
            farback_recv.at[a, m - 1],
            a * PER_APPLY + FARBACK + m - 1,
            up(2 * m),
        )

    def image_copy(a, d, h):
        mine = own[1][h].at[c] if a == 0 else second_image.at[c, halves[h], :]
        return remote(mine, mine, a * PER_APPLY + IMAGE + (SLAB - 1) * h + d - 1, beside(d))

    def dense_copy(d):
        return remote(
            dense_send.at[1, cluster(d)], dense_recv.at[d - 1], DENSE + d - 1, beside(d)
        )

    def dense_cross_copy(d):
        return remote(
            dense_send.at[0, cluster(d)],
            dense_recv.at[SLAB - 1 + d],
            DENSE + SLAB - 1 + d,
            across(d),
        )

    def each(count, act):
        def step(o, _):
            act(o)
            return 0

        lax.fori_loop(1, count + 1, step, 0)

    loads = [
        pltpu.make_async_copy(source, target, load_sem.at[at])
        for at, (source, target) in enumerate(
            (
                (charges_hbm, charges),
                (sizes_hbm, sizes_ref),
                (basis_hbm, basis_ref),
                (near_rows_hbm, near_rows_ref),
                (near_cols_hbm, near_cols_ref),
                (near_live_hbm, near_live_ref),
                (far_rows_hbm, far_rows_ref),
                (far_cols_hbm, far_cols_ref),
                (far_live_hbm, far_live_ref),
                (couplings_hbm, couplings),
                (blocks_hbm, blocks),
            )
        )
    ]
    for load in loads:
        load.start()

    coef_ahead[...] = jnp.zeros_like(coef_ahead)
    farback_recv[...] = jnp.zeros_like(farback_recv)

    @pl.when(jnp.logical_not(has_above))
    def _():
        for a in range(2):
            for h in range(2):
                ahead[a][h][...] = jnp.zeros_like(ahead[a][h])

    @pl.when(jnp.logical_not(has_below))
    def _():
        ahead_recv[...] = jnp.zeros_like(ahead_recv)

    barrier = pltpu.get_barrier_semaphore()

    def greet(device):
        pl.semaphore_signal(barrier, inc=1, device_id=device, device_id_type=MESH)

    for d in range(1, SLAB):
        greet(beside(d))
    for d in range(SLAB):
        greet(across(d))
    each(rows_above, lambda m: greet(up(2 * m)))
    each(rows_below, lambda m: greet(down(2 * m)))
    has_outer = jnp.where(odd == 1, r < n_rows - 1, r > 0)

    @pl.when(has_outer)
    def _():
        greet(up(jnp.where(odd == 1, 1, n_rows - 1)))


    def masked(values, size):
        panel = lax.broadcasted_iota(I32, values.shape, 1)
        return jnp.where(panel < size, values, jnp.zeros_like(values))

    def last_of(row, group):
        upto = order_s[row, group]
        before = jnp.where(group > 0, order_s[row, jnp.maximum(group - 1, 0)], 0)
        return jnp.maximum(upto - 1, 0), (upto > before).astype(F32)

    def set_coefficients(a, i):
        coef_own[a, ranks(i), :] = lax.dot_general(
            basis_ref[i],
            jnp.concatenate([own[a][0][i], own[a][1][i]], axis=0),
            (((1,), (1,)), ((), ())),
            preferred_element_type=F32,
        ).astype(BF16)

    def near_pass(a, order_row, forward, prefix, h):
        def slot(k, carry):
            total, previous = carry
            key = order_s[order_row, k]
            group = key >> 7
            other = (key >> 4) & 7
            source = own[a][h][other & 3]
            if forward:
                source = jnp.where(other < SLAB, source, ahead[a][h][other & 3])
            block = blocks[key & 15]
            product = lax.dot_general(
                source,
                block,
                (((1,), (1 if forward else 0,)), ((), ())),
                preferred_element_type=F32,
            )
            total = total * (group == previous).astype(F32) + product
            prefix[h, k] = total
            return total, group

        start = (jnp.zeros((HALF, PANELS), F32), jnp.int32(-1))
        lax.fori_loop(0, NEAR, slot, start, unroll=UNROLL)

    for load in loads[0:3]:
        load.wait()
    for i in range(SLAB):
        values = masked(charges[i], sizes_ref[i])
        for h in range(2):
            own[0][h][i] = values[halves[h]]
    set_coefficients(0, c)

    first = r * SLAB
    lane = lax.broadcasted_iota(I32, (1, LANES), 1)
    for load in loads[3:6]:
        load.wait()
    near_used = near_live_ref[0]
    by_row = jnp.broadcast_to((1 << 16) + lane, (1, LANES))
    by_col = by_row
    for s in range(NEAR):
        row = jnp.clip(near_rows_ref[s] - first, 0, SLAB - 1)
        col = jnp.clip(near_cols_ref[s] - first, 0, 2 * SLAB - 1)
        used = s < near_used
        row_key = (jnp.where(used, row, SLAB) << 7) + (col << 4) + s
        col_key = (jnp.where(used, col, 2 * SLAB) << 7) + (row << 4) + s
        by_row = jnp.where(lane == s, row_key, by_row)
        by_col = jnp.where(lane == s, col_key, by_col)
    for at, keys in enumerate((by_row, by_col)):
        ordered, laid = sort_keys(keys)
        order_v[2 * at : 2 * at + 1, :] = ordered
        order_v[2 * at + 1 : 2 * at + 2, :] = count_upto(laid, 7)
    order_v[4:8, :] = jnp.zeros((4, LANES), I32)
    share_order = pltpu.make_async_copy(order_v, order_s, load_sem.at[11])
    share_order.start()

    for load in loads[6:9]:
        load.wait()
    far_row = jnp.clip(far_rows_ref[...] - first, 0, SLAB - 1).reshape(1, LANES)
    far_col = jnp.clip(far_cols_ref[...] - first - SLAB, 0, REACH * SLAB - 1).reshape(1, LANES)
    far_slab = far_col >> 2
    far_tile = (far_slab >> 1) + jnp.where((far_slab & 1) == 1, TILES + odd, 0)
    far_key = (far_col & 3) * (2 * SLAB) + far_row
    far_key = jnp.where(lane < far_live_ref[0], far_key, -2 * SLAB)
    loads[9].wait()
    target = lax.broadcasted_iota(I32, (8 * SLAB, 2 * LANES), 0)
    chosen = jnp.where(target == jnp.concatenate([far_key, far_key + SLAB], axis=1), 1.0, 0.0)
    chosen = chosen.astype(BF16)
    in_slab = [
        jnp.broadcast_to(jnp.where(far_tile == o, 1.0, 0.0), (RANK, LANES)).astype(BF16)
        for o in range(2 * TILES)
    ]

    def dense_rows(m, _):
        halves = []
        for half in range(2):
            block = couplings[2 * m + half]
            tiles = [block * in_slab[o] for o in range(2 * TILES)]
            halves.append(jnp.concatenate(tiles, axis=0))
        rows = lax.dot_general(
            chosen,
            jnp.concatenate(halves, axis=1),
            (((1,), (1,)), ((), ())),
            preferred_element_type=F32,
        )
        for i in range(SLAB):
            dense_sum[i, pl.ds(pl.multiple_of(8 * m, 8), 8), :] = rows[8 * i : 8 * i + 8]
        return 0

    lax.fori_loop(0, RANK // 2, dense_rows, 0, unroll=4)
    pl.semaphore_wait(
        barrier, 2 * SLAB - 1 + rows_above + rows_below + jnp.where(has_outer, 1, 0)
    )

    for d in TURNS:
        i = cluster(d)
        dense_send[0, i] = dense_sum[i][:, :LANES].astype(BF16)
        dense_cross_copy(d).start()
        if d > 0:
            dense_send[1, i] = dense_sum[i][:, LANES:].astype(BF16)
            dense_copy(d).start()
    each(rows_below, lambda m: coef_copy(0, m).start())

    @pl.when(has_below)
    def _():
        for h in range(2):
            for turn in range(SLAB):
                field_copy(0, turn, h).start()

    for i in range(SLAB):

        @pl.when(i != c)
        def _():
            set_coefficients(0, i)

    sibling_copy().start()

    def own_tile(a):
        @pl.when(odd == 1)
        def _():
            coef_ahead[a, 0:RANK, :] = coef_own[a, ranks(c), :]

    own_tile(0)
    share_order.wait()
    loads[10].wait()

    def far_back(a):
        if a == 0:
            for d in TURNS:
                dense_cross_copy(d).wait_recv()
                if d > 0:
                    dense_copy(d).wait_recv()
            at = lax.broadcasted_iota(I32, (LANES, LANES), 0)
            wanted = (at & (RANK - 1)) * SLAB + (at >> 5)
            move = jnp.where(lax.broadcasted_iota(I32, (LANES, LANES), 1) == wanted, 1.0, 0.0)
            move = move.astype(BF16)
            total = dense_sum[c][:, LANES:]
            for d in range(SLAB - 1):
                total = total + dense_recv[d].astype(F32)
            dense[0:LANES, :] = jnp.dot(
                move, total.astype(BF16), preferred_element_type=F32
            ).astype(BF16)
            total = dense_recv[SLAB - 1].astype(F32)
            for d in range(1, SLAB):
                total = total + dense_recv[SLAB - 1 + d].astype(F32)
            dense[LANES:, :] = jnp.dot(
                move, total.astype(BF16), preferred_element_type=F32
            ).astype(BF16)
            sibling_copy().wait_recv()
        else:
            for d in TURNS:
                share_cross_copy(d).wait_recv()
                if d > 0:
                    share_copy(d).wait_recv()
        both = jnp.concatenate([coef_own[a], coef_sibling[a]], axis=0)
        farback_send[a] = lax.dot_general(
            dense[...], both, (((0,), (0,)), ((), ())), preferred_element_type=F32
        ).astype(BF16)
        each(rows_above, lambda m: farback_copy(a, m).start())

    def far_part(a):
        each(rows_above, lambda m: coef_copy(a, m).wait_recv())
        farpart_send[a] = jnp.dot(
            dense[...], coef_ahead[a], preferred_element_type=F32
        ).astype(BF16)
        for d in TURNS:
            farcross_copy(a, d).start()
            if d > 0:
                farpart_copy(a, d).start()

    def stage(a, at):
        if at == BACK_AT[a]:
            far_back(a)
        if at == PART_AT[a]:
            far_part(a)

    for a in range(2):
        for h in range(2):
            if a == 1:
                for d in (1, 3, 2):
                    image_copy(0, d, h).wait_recv()

                    @pl.when(has_below)
                    def _():
                        field_copy(1, d, h).start()

            near_pass(a, 2, False, back_prefix, h)

            @pl.when(has_above)
            def _():
                for turn in TURNS:
                    at, live = last_of(3, SLAB + cluster(turn))
                    ahead_send[a, turn, halves[h], :] = (back_prefix[h, at] * live).astype(BF16)
                    ahead_copy(a, turn, h).start()

            stage(a, h - 1)

        own_parts = []
        for h in range(2):
            @pl.when(has_above)
            def _():
                for turn in range(SLAB):
                    field_copy(a, turn, h).wait_recv()

            near_pass(a, 0, True, near_prefix, h)

            for turn in TURNS:
                i = cluster(turn)

                @pl.when(has_below)
                def _():
                    ahead_copy(a, turn, h).wait_recv()

                at, live = last_of(1, i)
                image = near_prefix[h, at] * live
                at, live = last_of(3, i)
                image = image + back_prefix[h, at] * live
                image = image + ahead_recv[a, turn, halves[h], :].astype(F32)
                if turn > 0:
                    part_send[a, turn - 1, halves[h], :] = image.astype(BF16)
                    part_copy(a, turn, h).start()
            own_parts.append(image)

            stage(a, 1 + h)

        far_total = farpart_send[a, ranks(c), :].astype(F32)
        far_total = far_total + jnp.where(odd == 1, farback_send[a, 0:RANK, :], 0).astype(F32)

        each(rows_below, lambda m: farback_copy(a, m).wait_recv())
        for m in range(TILES):
            far_total = far_total + farback_recv[a, m].astype(F32)
        for d in TURNS:
            farcross_copy(a, d).wait_recv()
            if d > 0:
                farpart_copy(a, d).wait_recv()
        for d in range(2 * SLAB - 1):
            far_total = far_total + farpart_recv[a, d].astype(F32)
        far_image = lax.dot_general(
            far_total.astype(BF16),
            basis_ref[c],
            (((0,), (0,)), ((), ())),
            preferred_element_type=F32,
        )
        for h in range(2):
            image = own_parts[h] + far_image[halves[h]]
            for d in TURNS[:3]:
                part_copy(a, d, h).wait_recv()
                image = image + part_recv[a, d - 1, halves[h], :].astype(F32)
            image = masked(image, sizes_ref[c]).astype(BF16)
            if a == 0:
                own[1][h][c] = image
            else:
                second_image[c, halves[h], :] = image
            for d in TURNS[:3]:
                image_copy(a, d, h).start()
            if a == 0:

                @pl.when(has_below)
                def _():
                    field_copy(1, 0, h).start()

        if a == 0:
            set_coefficients(1, c)
            for d in TURNS:
                share_cross_copy(d).start()
                if d > 0:
                    share_copy(d).start()
            each(rows_below, lambda m: coef_copy(1, m).start())
            own_tile(1)

    for h in range(2):
        first_image[:, halves[h], :] = own[1][h][...]
        for d in (1, 3, 2):
            image_copy(1, d, h).wait_recv()

    for a in range(2):
        for d in range(1, SLAB):
            farpart_copy(a, d).wait_send()
            for h in range(2):
                part_copy(a, d, h).wait_send()
                image_copy(a, d, h).wait_send()
        for d in range(SLAB):
            farcross_copy(a, d).wait_send()
        each(rows_below, lambda m: coef_copy(a, m).wait_send())
        each(rows_above, lambda m: farback_copy(a, m).wait_send())

        @pl.when(has_below)
        def _():
            for turn in range(SLAB):
                for h in range(2):
                    field_copy(a, turn, h).wait_send()

        @pl.when(has_above)
        def _():
            for turn in range(SLAB):
                for h in range(2):
                    ahead_copy(a, turn, h).wait_send()

    for d in range(1, SLAB):
        dense_copy(d).wait_send()
        share_copy(d).wait_send()
    sibling_copy().wait_send()
    for d in range(SLAB):
        dense_cross_copy(d).wait_send()
        share_cross_copy(d).wait_send()


def per_device(n_rows, *arrays):
    arrays = list(arrays)
    arrays[7] = jnp.transpose(arrays[7], (1, 2, 0))
    for n in range(11):
        if arrays[n].size > 1:
            arrays[n] = pltpu.with_memory_space_constraint(arrays[n], pltpu.HBM)
    hbm = pl.BlockSpec(memory_space=pltpu.HBM)
    vmem = pl.BlockSpec(memory_space=pltpu.VMEM)
    image = jax.ShapeDtypeStruct((SLAB, RHS, PANELS), BF16)
    return pl.pallas_call(
        functools.partial(kernel, n_rows),
        out_shape=(image, image),
        in_specs=[hbm] * 11,
        out_specs=(vmem, vmem),
        scratch_shapes=[
            pltpu.VMEM((SLAB, RHS, PANELS), BF16),
            pltpu.VMEM((SLAB, RANK, PANELS), BF16),
            pltpu.SMEM((SLAB,), I32),
            pltpu.VMEM((NEAR, PANELS, PANELS), BF16),
            pltpu.SMEM((NEAR,), I32),
            pltpu.SMEM((NEAR,), I32),
            pltpu.SMEM((1,), I32),
            pltpu.VMEM((RANK, RANK, FAR), BF16),
            pltpu.VMEM((FAR,), I32),
            pltpu.VMEM((FAR,), I32),
            pltpu.SMEM((1,), I32),
            pltpu.VMEM((SLAB, HALF, PANELS), BF16),
            pltpu.VMEM((SLAB, HALF, PANELS), BF16),
            pltpu.VMEM((SLAB, HALF, PANELS), BF16),
            pltpu.VMEM((SLAB, HALF, PANELS), BF16),
            pltpu.VMEM((SLAB, HALF, PANELS), BF16),
            pltpu.VMEM((SLAB, HALF, PANELS), BF16),
            pltpu.VMEM((SLAB, HALF, PANELS), BF16),
            pltpu.VMEM((SLAB, HALF, PANELS), BF16),
            pltpu.VMEM((8, LANES), I32),
            pltpu.SMEM((8, LANES), I32),
            pltpu.VMEM((2, SLAB * RANK, RHS), BF16),
            pltpu.VMEM((2, SLAB * RANK, RHS), BF16),
            pltpu.VMEM((2, TILES * RANK, RHS), BF16),
            pltpu.VMEM((SLAB, SLAB * RANK, 2 * LANES), F32),
            pltpu.VMEM((2, SLAB, SLAB * RANK, LANES), BF16),
            pltpu.VMEM((2 * SLAB - 1, SLAB * RANK, LANES), BF16),
            pltpu.VMEM((2 * SLAB * RANK, LANES), BF16),
            pltpu.VMEM((2, NEAR, HALF, PANELS), F32),
            pltpu.VMEM((2, NEAR, HALF, PANELS), F32),
            pltpu.VMEM((2, SLAB, RHS, PANELS), BF16),
            pltpu.VMEM((2, SLAB, RHS, PANELS), BF16),
            pltpu.VMEM((2, SLAB - 1, RHS, PANELS), BF16),
            pltpu.VMEM((2, SLAB - 1, RHS, PANELS), BF16),
            pltpu.VMEM((2, 2 * SLAB * RANK, RHS), BF16),
            pltpu.VMEM((2, 2 * SLAB - 1, RANK, RHS), BF16),
            pltpu.VMEM((2, TILES * RANK, RHS), BF16),
            pltpu.VMEM((2, TILES, RANK, RHS), BF16),
            pltpu.SemaphoreType.DMA((N_SEMS,)),
            pltpu.SemaphoreType.DMA((N_SEMS,)),
            pltpu.SemaphoreType.DMA((12,)),
        ],
        compiler_params=pltpu.CompilerParams(
            collective_id=0, has_side_effects=True, vmem_limit_bytes=40 * 1024 * 1024
        ),
    )(*arrays)


def solution(mesh):
    placed = (
        P("row", None, None),
        P("row", None, None),
        P("row"),
        P(("row", "col"), None, None),
        P(("row", "col")),
        P(("row", "col")),
        P(("row", "col")),
        P(("row", "col"), None, None),
        P(("row", "col")),
        P(("row", "col")),
        P(("row", "col")),
    )
    return jax.shard_map(
        functools.partial(per_device, mesh.shape["row"]),
        mesh=mesh,
        in_specs=placed,
        out_specs=(P("row", None, None), P("row", None, None)),
        check_vma=False,
    )
```

```python
import functools

import jax
import jax.numpy as jnp
from jax import lax
from jax.experimental import pallas as pl
from jax.experimental.pallas import tpu as pltpu
from jax.sharding import PartitionSpec as P

MESH = pl.DeviceIdType.MESH
F32 = jnp.float32
BF16 = jnp.bfloat16
I32 = jnp.int32

SLAB = 4
REACH = 7
TILES = 4
NEAR = 16
FAR = 128
RANK = 32
RHS = 128
PANELS = 256
LANES = 128
HALF = RHS // 2
UNROLL = 8
BACK_AT, PART_AT = (1, -1), (1, 0)

FIELD, AHEAD, PART, IMAGE, COEF, FARBACK, FARPART, SHARE, PER_APPLY = 0, 8, 16, 22, 28, 32, 36, 43, 50
DENSE = 2 * PER_APPLY
N_SEMS = DENSE + 7
TURNS = (2, 1, 3, 0)


def sort_keys(unique_keys):
    across = jnp.broadcast_to(unique_keys, (LANES, LANES))
    down = across.T
    rank = jnp.sum(jnp.where(across < down, 1, 0).astype(I32), axis=1, keepdims=True)
    lane = lax.broadcasted_iota(I32, (LANES, LANES), 1)
    ordered = jnp.sum(jnp.where(rank == lane, down, 0), axis=0, keepdims=True)
    return ordered, down


def count_upto(down, shift):
    lane = lax.broadcasted_iota(I32, (LANES, LANES), 1)
    return jnp.sum(jnp.where((down >> shift) <= lane, 1, 0).astype(I32), axis=0, keepdims=True)


def kernel(
    n_rows,
    charges_hbm,
    basis_hbm,
    sizes_hbm,
    blocks_hbm,
    near_rows_hbm,
    near_cols_hbm,
    near_live_hbm,
    couplings_hbm,
    far_rows_hbm,
    far_cols_hbm,
    far_live_hbm,
    first_image,
    second_image,
    charges,
    basis_ref,
    sizes_ref,
    blocks,
    near_rows_ref,
    near_cols_ref,
    near_live_ref,
    couplings,
    far_rows_ref,
    far_cols_ref,
    far_live_ref,
    masked_low,
    masked_high,
    own_low,
    own_high,
    next_first_low,
    next_first_high,
    next_second_low,
    next_second_high,
    order_v,
    order_s,
    coef_own,
    coef_sibling,
    coef_ahead,
    dense_sum,
    dense_send,
    dense_recv,
    dense,
    near_prefix,
    back_prefix,
    ahead_send,
    ahead_recv,
    part_send,
    part_recv,
    farpart_send,
    farpart_recv,
    farback_send,
    farback_recv,
    send_sem,
    recv_sem,
    load_sem,
):
    r = lax.axis_index("row")
    c = lax.axis_index("col")
    own = ((masked_low, masked_high), (own_low, own_high))
    ahead = ((next_first_low, next_first_high), (next_second_low, next_second_high))
    halves = (slice(0, HALF), slice(HALF, RHS))
    odd = lax.rem(r, 2)
    sibling = r + 1 - 2 * odd
    rows_above = jnp.minimum(TILES - odd, (n_rows - 1 - r) // 2)
    rows_below = jnp.minimum(TILES - odd, r // 2)
    has_above = r < n_rows - 1
    has_below = r > 0

    def up(o):
        return (lax.rem(r + o, n_rows), c)

    def down(o):
        return (lax.rem(r + n_rows - o, n_rows), c)

    def beside(d):
        return (r, lax.rem(c + d, SLAB))

    def across(d):
        return (sibling, lax.rem(c + d, SLAB))

    def cluster(turn):
        return lax.rem(c + turn, SLAB)

    def ranks(i):
        return pl.ds(pl.multiple_of(i * RANK, RANK), RANK)

    def remote(src, dst, at, device):
        return pltpu.make_async_remote_copy(
            src_ref=src,
            dst_ref=dst,
            send_sem=send_sem.at[at],
            recv_sem=recv_sem.at[at],
            device_id=device,
            device_id_type=MESH,
        )

    def field_copy(a, turn, h):
        i = cluster(SLAB - turn)
        at = a * PER_APPLY + FIELD + SLAB * h + turn
        return remote(own[a][h].at[i], ahead[a][h].at[i], at, down(1))

    def coef_copy(a, m):
        return remote(
            coef_own.at[a, ranks(c), :],
            coef_ahead.at[a, ranks(m - 1 + odd), :],
            a * PER_APPLY + COEF + m - 1,
            down(2 * m),
        )

    def sibling_copy():
        return remote(coef_own.at[0], coef_sibling.at[0], SHARE, across(0))

    def share_copy(d):
        mine = coef_own.at[1, ranks(c), :]
        return remote(mine, mine, PER_APPLY + SHARE + d - 1, beside(d))

    def share_cross_copy(d):
        return remote(
            coef_own.at[1, ranks(c), :],
            coef_sibling.at[1, ranks(c), :],
            PER_APPLY + SHARE + SLAB - 1 + d,
            across(d),
        )

    def ahead_copy(a, turn, h):
        return remote(
            ahead_send.at[a, turn, halves[h], :],
            ahead_recv.at[a, turn, halves[h], :],
            a * PER_APPLY + AHEAD + SLAB * h + turn,
            up(1),
        )

    def part_copy(a, d, h):
        return remote(
            part_send.at[a, d - 1, halves[h], :],
            part_recv.at[a, d - 1, halves[h], :],
            a * PER_APPLY + PART + (SLAB - 1) * h + d - 1,
            beside(d),
        )

    def farpart_copy(a, d):
        return remote(
            farpart_send.at[a, ranks(cluster(d)), :],
            farpart_recv.at[a, d - 1],
            a * PER_APPLY + FARPART + d - 1,
            beside(d),
        )

    def farcross_copy(a, d):
        return remote(
            farpart_send.at[a, ranks(SLAB + cluster(d)), :],
            farpart_recv.at[a, SLAB - 1 + d],
            a * PER_APPLY + FARPART + SLAB - 1 + d,
            across(d),
        )

    def farback_copy(a, m):
        return remote(
            farback_send.at[a, ranks(m - 1 + odd), :],
            farback_recv.at[a, m - 1],
            a * PER_APPLY + FARBACK + m - 1,
            up(2 * m),
        )

    def image_copy(a, d, h):
        mine = own[1][h].at[c] if a == 0 else second_image.at[c, halves[h], :]
        return remote(mine, mine, a * PER_APPLY + IMAGE + (SLAB - 1) * h + d - 1, beside(d))

    def dense_copy(d):
        return remote(
            dense_send.at[1, cluster(d)], dense_recv.at[d - 1], DENSE + d - 1, beside(d)
        )

    def dense_cross_copy(d):
        return remote(
            dense_send.at[0, cluster(d)],
            dense_recv.at[SLAB - 1 + d],
            DENSE + SLAB - 1 + d,
            across(d),
        )

    def each(count, act):
        def step(o, _):
            act(o)
            return 0

        lax.fori_loop(1, count + 1, step, 0)

    loads = [
        pltpu.make_async_copy(source, target, load_sem.at[at])
        for at, (source, target) in enumerate(
            (
                (charges_hbm, charges),
                (sizes_hbm, sizes_ref),
                (basis_hbm, basis_ref),
                (near_rows_hbm, near_rows_ref),
                (near_cols_hbm, near_cols_ref),
                (near_live_hbm, near_live_ref),
                (far_rows_hbm, far_rows_ref),
                (far_cols_hbm, far_cols_ref),
                (far_live_hbm, far_live_ref),
                (couplings_hbm, couplings),
                (blocks_hbm, blocks),
            )
        )
    ]
    for load in loads:
        load.start()

    coef_ahead[...] = jnp.zeros_like(coef_ahead)
    farback_recv[...] = jnp.zeros_like(farback_recv)

    @pl.when(jnp.logical_not(has_above))
    def _():
        for a in range(2):
            for h in range(2):
                ahead[a][h][...] = jnp.zeros_like(ahead[a][h])

    @pl.when(jnp.logical_not(has_below))
    def _():
        ahead_recv[...] = jnp.zeros_like(ahead_recv)

    barrier = pltpu.get_barrier_semaphore()

    def greet(device):
        pl.semaphore_signal(barrier, inc=1, device_id=device, device_id_type=MESH)

    for d in range(1, SLAB):
        greet(beside(d))
    for d in range(SLAB):
        greet(across(d))
    each(rows_above, lambda m: greet(up(2 * m)))
    each(rows_below, lambda m: greet(down(2 * m)))
    has_outer = jnp.where(odd == 1, r < n_rows - 1, r > 0)

    @pl.when(has_outer)
    def _():
        greet(up(jnp.where(odd == 1, 1, n_rows - 1)))


    def masked(values, size):
        panel = lax.broadcasted_iota(I32, values.shape, 1)
        return jnp.where(panel < size, values, jnp.zeros_like(values))

    def last_of(row, group):
        upto = order_s[row, group]
        before = jnp.where(group > 0, order_s[row, jnp.maximum(group - 1, 0)], 0)
        return jnp.maximum(upto - 1, 0), (upto > before).astype(F32)

    def set_coefficients(a, i):
        coef_own[a, ranks(i), :] = lax.dot_general(
            basis_ref[i],
            jnp.concatenate([own[a][0][i], own[a][1][i]], axis=0),
            (((1,), (1,)), ((), ())),
            preferred_element_type=F32,
        ).astype(BF16)

    def near_pass(a, order_row, forward, prefix, h):
        def slot(k, carry):
            total, previous = carry
            key = order_s[order_row, k]
            group = key >> 7
            other = (key >> 4) & 7
            source = own[a][h][other & 3]
            if forward:
                source = jnp.where(other < SLAB, source, ahead[a][h][other & 3])
            block = blocks[key & 15]
            product = lax.dot_general(
                source,
                block,
                (((1,), (1 if forward else 0,)), ((), ())),
                preferred_element_type=F32,
            )
            total = total * (group == previous).astype(F32) + product
            prefix[h, k] = total
            return total, group

        start = (jnp.zeros((HALF, PANELS), F32), jnp.int32(-1))
        lax.fori_loop(0, NEAR, slot, start, unroll=UNROLL)

    for load in loads[0:3]:
        load.wait()
    for i in range(SLAB):
        values = masked(charges[i], sizes_ref[i])
        for h in range(2):
            own[0][h][i] = values[halves[h]]
    set_coefficients(0, c)

    first = r * SLAB
    lane = lax.broadcasted_iota(I32, (1, LANES), 1)
    for load in loads[3:6]:
        load.wait()
    near_used = near_live_ref[0]
    by_row = jnp.broadcast_to((1 << 16) + lane, (1, LANES))
    by_col = by_row
    for s in range(NEAR):
        row = jnp.clip(near_rows_ref[s] - first, 0, SLAB - 1)
        col = jnp.clip(near_cols_ref[s] - first, 0, 2 * SLAB - 1)
        used = s < near_used
        row_key = (jnp.where(used, row, SLAB) << 7) + (col << 4) + s
        col_key = (jnp.where(used, col, 2 * SLAB) << 7) + (row << 4) + s
        by_row = jnp.where(lane == s, row_key, by_row)
        by_col = jnp.where(lane == s, col_key, by_col)
    for at, keys in enumerate((by_row, by_col)):
        ordered, laid = sort_keys(keys)
        order_v[2 * at : 2 * at + 1, :] = ordered
        order_v[2 * at + 1 : 2 * at + 2, :] = count_upto(laid, 7)
    order_v[4:8, :] = jnp.zeros((4, LANES), I32)
    share_order = pltpu.make_async_copy(order_v, order_s, load_sem.at[11])
    share_order.start()

    for load in loads[6:9]:
        load.wait()
    far_row = jnp.clip(far_rows_ref[...] - first, 0, SLAB - 1).reshape(1, LANES)
    far_col = jnp.clip(far_cols_ref[...] - first - SLAB, 0, REACH * SLAB - 1).reshape(1, LANES)
    far_slab = far_col >> 2
    far_tile = (far_slab >> 1) + jnp.where((far_slab & 1) == 1, TILES + odd, 0)
    far_key = (far_col & 3) * (2 * SLAB) + far_row
    far_key = jnp.where(lane < far_live_ref[0], far_key, -2 * SLAB)
    loads[9].wait()
    target = lax.broadcasted_iota(I32, (8 * SLAB, 2 * LANES), 0)
    chosen = jnp.where(target == jnp.concatenate([far_key, far_key + SLAB], axis=1), 1.0, 0.0)
    chosen = chosen.astype(BF16)
    in_slab = [
        jnp.broadcast_to(jnp.where(far_tile == o, 1.0, 0.0), (RANK, LANES)).astype(BF16)
        for o in range(2 * TILES)
    ]

    def dense_rows(m, _):
        halves = []
        for half in range(2):
            block = couplings[2 * m + half]
            tiles = [block * in_slab[o] for o in range(2 * TILES)]
            halves.append(jnp.concatenate(tiles, axis=0))
        rows = lax.dot_general(
            chosen,
            jnp.concatenate(halves, axis=1),
            (((1,), (1,)), ((), ())),
            preferred_element_type=F32,
        )
        for i in range(SLAB):
            dense_sum[i, pl.ds(pl.multiple_of(8 * m, 8), 8), :] = rows[8 * i : 8 * i + 8]
        return 0

    lax.fori_loop(0, RANK // 2, dense_rows, 0, unroll=4)
    pl.semaphore_wait(
        barrier, 2 * SLAB - 1 + rows_above + rows_below + jnp.where(has_outer, 1, 0)
    )

    for d in TURNS:
        i = cluster(d)
        dense_send[0, i] = dense_sum[i][:, :LANES].astype(BF16)
        dense_cross_copy(d).start()
        if d > 0:
            dense_send[1, i] = dense_sum[i][:, LANES:].astype(BF16)
            dense_copy(d).start()
    each(rows_below, lambda m: coef_copy(0, m).start())

    @pl.when(has_below)
    def _():
        for h in range(2):
            for turn in range(SLAB):
                field_copy(0, turn, h).start()

    for i in range(SLAB):

        @pl.when(i != c)
        def _():
            set_coefficients(0, i)

    sibling_copy().start()

    def own_tile(a):
        @pl.when(odd == 1)
        def _():
            coef_ahead[a, 0:RANK, :] = coef_own[a, ranks(c), :]

    own_tile(0)
    share_order.wait()
    loads[10].wait()

    def far_back(a):
        if a == 0:
            for d in TURNS:
                dense_cross_copy(d).wait_recv()
                if d > 0:
                    dense_copy(d).wait_recv()
            at = lax.broadcasted_iota(I32, (LANES, LANES), 0)
            wanted = (at & (RANK - 1)) * SLAB + (at >> 5)
            move = jnp.where(lax.broadcasted_iota(I32, (LANES, LANES), 1) == wanted, 1.0, 0.0)
            move = move.astype(BF16)
            total = dense_sum[c][:, LANES:]
            for d in range(SLAB - 1):
                total = total + dense_recv[d].astype(F32)
            dense[0:LANES, :] = jnp.dot(
                move, total.astype(BF16), preferred_element_type=F32
            ).astype(BF16)
            total = dense_recv[SLAB - 1].astype(F32)
            for d in range(1, SLAB):
                total = total + dense_recv[SLAB - 1 + d].astype(F32)
            dense[LANES:, :] = jnp.dot(
                move, total.astype(BF16), preferred_element_type=F32
            ).astype(BF16)
            sibling_copy().wait_recv()
        else:
            for d in TURNS:
                share_cross_copy(d).wait_recv()
                if d > 0:
                    share_copy(d).wait_recv()
        both = jnp.concatenate([coef_own[a], coef_sibling[a]], axis=0)
        farback_send[a] = lax.dot_general(
            dense[...], both, (((0,), (0,)), ((), ())), preferred_element_type=F32
        ).astype(BF16)
        each(rows_above, lambda m: farback_copy(a, m).start())

    def far_part(a):
        each(rows_above, lambda m: coef_copy(a, m).wait_recv())
        farpart_send[a] = jnp.dot(
            dense[...], coef_ahead[a], preferred_element_type=F32
        ).astype(BF16)
        for d in TURNS:
            farcross_copy(a, d).start()
            if d > 0:
                farpart_copy(a, d).start()

    def stage(a, at):
        if at == BACK_AT[a]:
            far_back(a)
        if at == PART_AT[a]:
            far_part(a)

    def finish_early(a):
        each(rows_below, lambda m: coef_copy(a, m).wait_send())
        each(rows_above, lambda m: farback_copy(a, m).wait_send())

        @pl.when(has_below)
        def _():
            for turn in range(SLAB):
                for h in range(2):
                    field_copy(a, turn, h).wait_send()

        @pl.when(has_above)
        def _():
            for turn in range(SLAB):
                for h in range(2):
                    ahead_copy(a, turn, h).wait_send()

    def finish_parts(a):
        for d in range(1, SLAB):
            farpart_copy(a, d).wait_send()
            for h in range(2):
                part_copy(a, d, h).wait_send()
        for d in range(SLAB):
            farcross_copy(a, d).wait_send()

    for a in range(2):
        for h in range(2):
            if a == 1:
                for d in (1, 3, 2):
                    image_copy(0, d, h).wait_recv()

                    @pl.when(has_below)
                    def _():
                        field_copy(1, d, h).start()

            near_pass(a, 2, False, back_prefix, h)

            @pl.when(has_above)
            def _():
                for turn in TURNS:
                    at, live = last_of(3, SLAB + cluster(turn))
                    ahead_send[a, turn, halves[h], :] = (back_prefix[h, at] * live).astype(BF16)
                    ahead_copy(a, turn, h).start()

            stage(a, h - 1)

        own_parts = []
        for h in range(2):
            @pl.when(has_above)
            def _():
                for turn in range(SLAB):
                    field_copy(a, turn, h).wait_recv()

            near_pass(a, 0, True, near_prefix, h)

            for turn in TURNS:
                i = cluster(turn)

                @pl.when(has_below)
                def _():
                    ahead_copy(a, turn, h).wait_recv()

                at, live = last_of(1, i)
                image = near_prefix[h, at] * live
                at, live = last_of(3, i)
                image = image + back_prefix[h, at] * live
                image = image + ahead_recv[a, turn, halves[h], :].astype(F32)
                if turn > 0:
                    part_send[a, turn - 1, halves[h], :] = image.astype(BF16)
                    part_copy(a, turn, h).start()
            own_parts.append(image)

            stage(a, 1 + h)

        far_total = farpart_send[a, ranks(c), :].astype(F32)
        far_total = far_total + jnp.where(odd == 1, farback_send[a, 0:RANK, :], 0).astype(F32)

        if a == 1:
            for h in range(2):
                first_image[:, halves[h], :] = own[1][h][...]
                for d in range(1, SLAB):
                    image_copy(0, d, h).wait_send()
            for d in range(1, SLAB):
                dense_copy(d).wait_send()
                share_copy(d).wait_send()
            for d in range(SLAB):
                dense_cross_copy(d).wait_send()
                share_cross_copy(d).wait_send()
            sibling_copy().wait_send()
            finish_early(0)
            finish_parts(0)
            finish_early(1)

        each(rows_below, lambda m: farback_copy(a, m).wait_recv())
        for m in range(TILES):
            far_total = far_total + farback_recv[a, m].astype(F32)
        for d in TURNS:
            farcross_copy(a, d).wait_recv()
            if d > 0:
                farpart_copy(a, d).wait_recv()
        for d in range(2 * SLAB - 1):
            far_total = far_total + farpart_recv[a, d].astype(F32)
        far_image = lax.dot_general(
            far_total.astype(BF16),
            basis_ref[c],
            (((0,), (0,)), ((), ())),
            preferred_element_type=F32,
        )
        for h in range(2):
            image = own_parts[h] + far_image[halves[h]]
            for d in TURNS[:3]:
                part_copy(a, d, h).wait_recv()
                image = image + part_recv[a, d - 1, halves[h], :].astype(F32)
            image = masked(image, sizes_ref[c]).astype(BF16)
            if a == 0:
                own[1][h][c] = image
            else:
                second_image[c, halves[h], :] = image
            for d in TURNS[:3]:
                image_copy(a, d, h).start()
            if a == 0:

                @pl.when(has_below)
                def _():
                    field_copy(1, 0, h).start()

        if a == 0:
            set_coefficients(1, c)
            for d in TURNS:
                share_cross_copy(d).start()
                if d > 0:
                    share_copy(d).start()
            each(rows_below, lambda m: coef_copy(1, m).start())
            own_tile(1)

    finish_parts(1)
    for h in range(2):
        for d in (1, 3, 2):
            image_copy(1, d, h).wait_recv()

    for h in range(2):
        for d in range(1, SLAB):
            image_copy(1, d, h).wait_send()


def per_device(n_rows, *arrays):
    arrays = list(arrays)
    arrays[7] = jnp.transpose(arrays[7], (1, 2, 0))
    for n in range(11):
        if arrays[n].size > 1:
            arrays[n] = pltpu.with_memory_space_constraint(arrays[n], pltpu.HBM)
    hbm = pl.BlockSpec(memory_space=pltpu.HBM)
    vmem = pl.BlockSpec(memory_space=pltpu.VMEM)
    image = jax.ShapeDtypeStruct((SLAB, RHS, PANELS), BF16)
    return pl.pallas_call(
        functools.partial(kernel, n_rows),
        out_shape=(image, image),
        in_specs=[hbm] * 11,
        out_specs=(vmem, vmem),
        scratch_shapes=[
            pltpu.VMEM((SLAB, RHS, PANELS), BF16),
            pltpu.VMEM((SLAB, RANK, PANELS), BF16),
            pltpu.SMEM((SLAB,), I32),
            pltpu.VMEM((NEAR, PANELS, PANELS), BF16),
            pltpu.SMEM((NEAR,), I32),
            pltpu.SMEM((NEAR,), I32),
            pltpu.SMEM((1,), I32),
            pltpu.VMEM((RANK, RANK, FAR), BF16),
            pltpu.VMEM((FAR,), I32),
            pltpu.VMEM((FAR,), I32),
            pltpu.SMEM((1,), I32),
            pltpu.VMEM((SLAB, HALF, PANELS), BF16),
            pltpu.VMEM((SLAB, HALF, PANELS), BF16),
            pltpu.VMEM((SLAB, HALF, PANELS), BF16),
            pltpu.VMEM((SLAB, HALF, PANELS), BF16),
            pltpu.VMEM((SLAB, HALF, PANELS), BF16),
            pltpu.VMEM((SLAB, HALF, PANELS), BF16),
            pltpu.VMEM((SLAB, HALF, PANELS), BF16),
            pltpu.VMEM((SLAB, HALF, PANELS), BF16),
            pltpu.VMEM((8, LANES), I32),
            pltpu.SMEM((8, LANES), I32),
            pltpu.VMEM((2, SLAB * RANK, RHS), BF16),
            pltpu.VMEM((2, SLAB * RANK, RHS), BF16),
            pltpu.VMEM((2, TILES * RANK, RHS), BF16),
            pltpu.VMEM((SLAB, SLAB * RANK, 2 * LANES), F32),
            pltpu.VMEM((2, SLAB, SLAB * RANK, LANES), BF16),
            pltpu.VMEM((2 * SLAB - 1, SLAB * RANK, LANES), BF16),
            pltpu.VMEM((2 * SLAB * RANK, LANES), BF16),
            pltpu.VMEM((2, NEAR, HALF, PANELS), F32),
            pltpu.VMEM((2, NEAR, HALF, PANELS), F32),
            pltpu.VMEM((2, SLAB, RHS, PANELS), BF16),
            pltpu.VMEM((2, SLAB, RHS, PANELS), BF16),
            pltpu.VMEM((2, SLAB - 1, RHS, PANELS), BF16),
            pltpu.VMEM((2, SLAB - 1, RHS, PANELS), BF16),
            pltpu.VMEM((2, 2 * SLAB * RANK, RHS), BF16),
            pltpu.VMEM((2, 2 * SLAB - 1, RANK, RHS), BF16),
            pltpu.VMEM((2, TILES * RANK, RHS), BF16),
            pltpu.VMEM((2, TILES, RANK, RHS), BF16),
            pltpu.SemaphoreType.DMA((N_SEMS,)),
            pltpu.SemaphoreType.DMA((N_SEMS,)),
            pltpu.SemaphoreType.DMA((12,)),
        ],
        compiler_params=pltpu.CompilerParams(
            collective_id=0, has_side_effects=True, vmem_limit_bytes=40 * 1024 * 1024
        ),
    )(*arrays)


def solution(mesh):
    placed = (
        P("row", None, None),
        P("row", None, None),
        P("row"),
        P(("row", "col"), None, None),
        P(("row", "col")),
        P(("row", "col")),
        P(("row", "col")),
        P(("row", "col"), None, None),
        P(("row", "col")),
        P(("row", "col")),
        P(("row", "col")),
    )
    return jax.shard_map(
        functools.partial(per_device, mesh.shape["row"]),
        mesh=mesh,
        in_specs=placed,
        out_specs=(P("row", None, None), P("row", None, None)),
        check_vma=False,
    )
```
